128 devices in a mesh: context: 16 (over x, y_lo, core), fsdp: 8 (over z, y_hi).
Axes of the slice: x: 4, y: 4 (y_hi: 2, y_lo: 2; y = y_hi * 2 + y_lo), z: 4, core: 2. Of those that a mesh axis runs over, the one named last changes fastest.
Arguments:
- inputs: bfloat16 [8, 2048, 1536], P('fsdp', 'context'), may hold values from -6 to 6
- segments: int32 [8, 2048], P('fsdp', 'context'), may hold values from 0 to 2, as said below
- gain_attn: bfloat16 [1536], P('fsdp'), may hold values from 0.5 to 1.5
- w_query: bfloat16 [1536, 1536], P('fsdp'), may hold values from -0.15625 to 0.15625
- b_query: bfloat16 [1536], P('fsdp'), may hold values from -3 to 3
- w_key: bfloat16 [1536, 256], P('fsdp'), may hold values from -0.15625 to 0.15625
- b_key: bfloat16 [256], P('fsdp'), may hold values from -3 to 3
- w_value: bfloat16 [1536, 256], P('fsdp'), may hold values from -0.15625 to 0.15625
- b_value: bfloat16 [256], P('fsdp'), may hold values from -3 to 3
- w_output: bfloat16 [1536, 1536], P('fsdp'), may hold values from -0.625 to 0.625
- gain_mlp: bfloat16 [1536], P('fsdp'), may hold values from 0.5 to 1.5
- w_gate: bfloat16 [1536, 8960], P('fsdp'), may hold values from -0.15625 to 0.15625
- w_up: bfloat16 [1536, 8960], P('fsdp'), may hold values from -0.15625 to 0.15625
- w_down: bfloat16 [8960, 1536], P('fsdp'), may hold values from -0.09375 to 0.09375
- cotangent: bfloat16 [8, 2048, 1536], P('fsdp', 'context'), may hold values from -6 to 6
Outputs:
- output: bfloat16 [8, 2048, 1536], P('fsdp', 'context')
- grad_inputs: bfloat16 [8, 2048, 1536], P('fsdp', 'context')
- grad_gain_attn: float32 [1536], P('fsdp')
- grad_w_query: float32 [1536, 1536], P('fsdp')
- grad_b_query: float32 [1536], P('fsdp')
- grad_w_key: float32 [1536, 256], P('fsdp')
- grad_b_key: float32 [256], P('fsdp')
- grad_w_value: float32 [1536, 256], P('fsdp')
- grad_b_value: float32 [256], P('fsdp')
- grad_w_output: float32 [1536, 1536], P('fsdp')
- grad_gain_mlp: float32 [1536], P('fsdp')
- grad_w_gate: float32 [1536, 8960], P('fsdp')
- grad_w_up: float32 [1536, 8960], P('fsdp')
- grad_w_down: float32 [8960, 1536], P('fsdp')
The draws below stay inside these ranges and needn't reach their ends.
Inputs may be any that keep to these rules, and one draw needn't show every extreme that they name: `segments`: in every sequence the numbers never fall and start at 0; each sequence holds three documents, each of 204 tokens or more.
All inputs are finite; a program needn't handle non-finite values.
Results may differ from the reference program's by a relative error of at most 0.025.
Values may be sent and summed in bfloat16 or wider, within the bound.
No kernel may reach another device: no remote copies, remote signals or barrier semaphores. Data moves between devices by JAX's collectives and lax.ppermute only.
A program may use at most 384 MiB of HBM per device.

```python
import math
import jax
import jax.numpy as jnp
from jax import lax

D = 1536
FF = 8960
HEADS = 12
KV_HEADS = 2
HEAD = 128
SEQ_LEN = 2048
SEQS = 8
KVW = 256


def draw_segments(key, part):
    key = jax.random.fold_in(key, 11)
    key_one, key_two = jax.random.split(key, 2)
    tenth = SEQ_LEN // 10
    first_cut = jax.random.randint(key_one, (SEQS, 1), tenth, 2 * tenth + 1)
    long_length = jax.random.randint(key_two, (SEQS, 1), SEQ_LEN * 11 // 20, SEQ_LEN * 7 // 10 + 1)
    second_cut = first_cut + long_length
    places = jnp.arange(SEQ_LEN, dtype=jnp.int32)[None, :]
    numbers = (places >= first_cut).astype(jnp.int32) + (places >= second_cut).astype(jnp.int32)
    return numbers.astype(jnp.int32)


def levels(stream_key, shape, cuts, low, high):
    level = 1.0
    for axis_at, shards_of in cuts:
        steps = jax.random.uniform(jax.random.fold_in(jax.random.fold_in(stream_key, 6), axis_at), (shards_of,), jnp.float32, low / len(cuts), high / len(cuts))
        level = level * jnp.repeat(jnp.exp(steps), shape[axis_at] // shards_of).reshape((-1,) + (1,) * (len(shape) - 1 - axis_at))
    return level


def scatter_about(rng, shape, spread, bound, shards=(), kind=jnp.bfloat16):
    drawn = spread * jax.random.normal(rng, shape, jnp.float32)
    if shards:
        drawn = drawn * levels(rng, shape, shards, -0.22, 0.18)
    return jnp.clip(drawn, -bound, bound).astype(kind)


def setup_inputs(seed: int = 0) -> dict:
    splits = jax.random.split(jax.random.key(seed), 16)
    inputs = scatter_about(splits[0], (SEQS, SEQ_LEN, D), 1.0, 6.0, ((0, 8), (1, 16)))
    segments = draw_segments(jax.random.fold_in(splits[15], 71), 0)
    gain_attn = jnp.clip(1.0 + 0.1 * jax.random.normal(splits[2], (D,), jnp.float32), 0.5, 1.5).astype(jnp.bfloat16)
    w_query = scatter_about(splits[3], (D, D), D ** -0.5, 0.15625, ((0, 8),))
    b_query = scatter_about(splits[4], (D,), 0.5, 3.0, ((0, 8),))
    w_key = scatter_about(splits[5], (D, KVW), D ** -0.5, 0.15625, ((0, 8),))
    b_key = scatter_about(splits[6], (KVW,), 0.5, 3.0, ((0, 8),))
    w_value = scatter_about(splits[7], (D, KVW), D ** -0.5, 0.15625, ((0, 8),))
    b_value = scatter_about(splits[8], (KVW,), 0.5, 3.0, ((0, 8),))
    w_output = scatter_about(splits[9], (D, D), (D // 16) ** -0.5, 0.625, ((0, 8),))
    gain_mlp = jnp.clip(1.0 + 0.1 * jax.random.normal(splits[10], (D,), jnp.float32), 0.5, 1.5).astype(jnp.bfloat16)
    w_gate = scatter_about(splits[11], (D, FF), D ** -0.5, 0.15625, ((0, 8),))
    w_up = scatter_about(splits[12], (D, FF), D ** -0.5, 0.15625, ((0, 8),))
    w_down = scatter_about(splits[13], (FF, D), (FF // 2) ** -0.5, 0.09375, ((0, 8),))
    cotangent = scatter_about(splits[14], (SEQS, SEQ_LEN, D), 1.0, 6.0, ((0, 8), (1, 16)))
    return {"inputs": inputs, "segments": segments, "gain_attn": gain_attn, "w_query": w_query, "b_query": b_query, "w_key": w_key, "b_key": b_key, "w_value": w_value, "b_value": b_value, "w_output": w_output, "gain_mlp": gain_mlp, "w_gate": w_gate, "w_up": w_up, "w_down": w_down, "cotangent": cotangent}


@jax.custom_vjp
def low(v):
    return lax.optimization_barrier(v.astype(jnp.bfloat16)).astype(jnp.float32)

@jax.custom_vjp
def low_back(v):
    return v

def low_keep(v):
    return (low(v), None)

def low_pass(kept, grad):
    return (grad,)

def back_keep(v):
    return (v, None)

def back_low(kept, grad):
    return (low(grad),)
low.defvjp(low_keep, low_pass)
low_back.defvjp(back_keep, back_low)
EPS = 1e-06
THETA = 1000000.0
HIGH = lax.Precision.HIGHEST

def rms_norm(values, gain):
    return values * lax.rsqrt(lax.optimization_barrier(jnp.mean(values * values, axis=-1, keepdims=True)) + EPS) * gain

def rope_tables(positions):
    half_width = HEAD // 2
    freqs = THETA ** (-(jnp.arange(half_width, dtype=jnp.float32) * 2.0 / HEAD))
    angle = positions.astype(jnp.float32)[:, None] * freqs[None, :]
    return (jnp.cos(angle), jnp.sin(angle))

def rotate(values, cosine_table, sine_table, direction):
    half_width = HEAD // 2
    first_half = values[..., :half_width]
    second_half = values[..., half_width:]
    cosine_part = cosine_table[:, None, :]
    sine_part = sine_table[:, None, :] * direction
    return jnp.concatenate([first_half * cosine_part - second_half * sine_part, second_half * cosine_part + first_half * sine_part], axis=-1)

def project(left, right):
    return jnp.dot(left, right, precision=HIGH)

def layer(tokens, doc_ids, gain_attn, w_query, b_query, w_key, b_key, w_value, b_value, w_output, gain_mlp, w_gate, w_up, w_down):
    seq_length = tokens.shape[0]
    places = jnp.arange(seq_length, dtype=jnp.int32)
    begins = lax.optimization_barrier(jnp.sum((doc_ids[None, :] < doc_ids[:, None]).astype(jnp.int32), axis=1))
    cosine_table, sine_table = rope_tables(places - begins)
    normed_one = low(rms_norm(tokens, gain_attn))
    queries = low_back(project(normed_one, w_query) + b_query).reshape(seq_length, HEADS, HEAD)
    keys = low_back(project(normed_one, w_key) + b_key).reshape(seq_length, KV_HEADS, HEAD)
    values = low(low_back(project(normed_one, w_value) + b_value)).reshape(seq_length, KV_HEADS, HEAD)
    turned_q = low(rotate(queries, cosine_table, sine_table, 1.0))
    turned_k = low(rotate(keys, cosine_table, sine_table, 1.0))
    group = HEADS // KV_HEADS
    block = math.gcd(seq_length, 512)
    blocks = seq_length // block
    score_scale = 1.0 / math.sqrt(HEAD)

    @jax.checkpoint
    def attend(item):
        block_q, block_ids, block_places = item
        scores = jnp.einsum('qkgd,skd->kgqs', block_q, turned_k, precision=HIGH) * score_scale
        scores = low_back(scores)
        visible = (block_ids[:, None] == doc_ids[None, :]) & (block_places[:, None] >= places[None, :])
        scores = jnp.where(visible[None, None], scores, -1e+30)
        weights = low(jax.nn.softmax(scores, axis=-1))
        return jnp.einsum('kgqs,skd->qkgd', weights, values, precision=HIGH)
    mixed = lax.map(attend, (turned_q.reshape(blocks, block, KV_HEADS, group, HEAD), doc_ids.reshape(blocks, block), places.reshape(blocks, block)))
    attended = low(low_back(mixed.reshape(seq_length, D)))
    residual = tokens + low_back(project(attended, w_output))
    normed_two = low(rms_norm(residual, gain_mlp))
    gate = low_back(project(normed_two, w_gate))
    upward = low_back(project(normed_two, w_up))
    hidden = low(jax.nn.silu(gate) * upward)
    return residual + low_back(project(hidden, w_down))

def reference(inputs, segments, gain_attn, w_query, b_query, w_key, b_key, w_value, b_value, w_output, gain_mlp, w_gate, w_up, w_down, cotangent):
    weights = tuple((item.astype(jnp.float32) for item in (gain_attn, w_query, b_query, w_key, b_key, w_value, b_value, w_output, gain_mlp, w_gate, w_up, w_down)))

    def forward(tokens, *params):

        def one_sequence(item):
            return layer(item[0], item[1], *params)
        return lax.map(one_sequence, (tokens, segments))
    result, pull = jax.vjp(forward, inputs.astype(jnp.float32), *weights)
    grads = pull(cotangent.astype(jnp.float32))
    return (result.astype(jnp.bfloat16), grads[0].astype(jnp.bfloat16), grads[1], grads[2], grads[3], grads[4], grads[5], grads[6], grads[7], grads[8], grads[9], grads[10], grads[11], grads[12])
```

```python
import functools
import math

import jax
import jax.numpy as jnp
import numpy as np
from jax import lax
from jax.experimental import pallas as pl
from jax.experimental.pallas import tpu as pltpu
from jax.sharding import PartitionSpec as P

D = 1536
FF = 8960
HEADS = 12
KV_HEADS = 2
HEAD = 128
SEQ = 2048
EPS = 1e-06
THETA = 1000000.0
NCTX, NFS = 16, 8
TOK = SEQ // NCTX
ROWS = D // NFS
SLICE = FF // NCTX
SLOT = 640
PIECE = 80
AXES = ("context", "fsdp")
SCALE = 1.0 / math.sqrt(HEAD)
BQ, BK = 256, 512
BF, F32 = jnp.bfloat16, jnp.float32
VMEM_BYTES = 56 * 1024 * 1024
NEG = -1e30


def split_place(c, f):
    return c // 4, (c // 2) % 2, c % 2, f // 2, f % 2


def pairs_of(move):
    pairs = []
    for c in range(NCTX):
        for f in range(NFS):
            x, yl, core, z, yh = move(*split_place(c, f))
            pairs.append((c * NFS + f, ((x % 4) * 4 + (yl % 2) * 2 + core % 2) * NFS + (z % 4) * 2 + yh % 2))
    return pairs


MOVES = {
    "x+": pairs_of(lambda x, yl, core, z, yh: (x + 1, yl, core, z, yh)),
    "x-": pairs_of(lambda x, yl, core, z, yh: (x - 1, yl, core, z, yh)),
    "yl": pairs_of(lambda x, yl, core, z, yh: (x, yl + 1, core, z, yh)),
    "core": pairs_of(lambda x, yl, core, z, yh: (x, yl, core + 1, z, yh)),
    "z+": pairs_of(lambda x, yl, core, z, yh: (x, yl, core, z + 1, yh)),
    "z-": pairs_of(lambda x, yl, core, z, yh: (x, yl, core, z - 1, yh)),
    "yw": pairs_of(lambda x, yl, core, z, yh: (x, yl + 1, core, z, yh + 1)),
}


def down_owner():
    pairs = []
    for c in range(NCTX):
        for f in range(NFS):
            s = c ^ (2 * (f % 2))
            pairs.append((c * NFS + f, ((s % 2) * 8 + f) * NFS + s // 2))
    return pairs


TO_OWNER = down_owner()
FROM_OWNER = [(b, a) for a, b in TO_OWNER]


def send(value, move):
    pairs = MOVES[move] if isinstance(move, str) else move
    return lax.ppermute(value, AXES, pairs)


REL8 = [(0, 0), (-1, 0), (1, 0), (0, 1), (-1, 1), (2, 0), (1, 1), (2, 1)]


def gather8(v, plus, minus, pair):
    a, b, c = send(v, plus), send(v, minus), send(v, pair)
    d, e, f = send(c, plus), send(b, minus), send(b, pair)
    g = send(e, pair)
    return [v, a, b, c, d, e, f, g]


def add(*terms):
    total = terms[0].astype(F32)
    for t in terms[1:]:
        total = total + t.astype(F32)
    return total


def scatter8(q, plus, minus, pair):
    g1 = send(q[7], pair)
    d1 = send(q[4], minus)
    f1 = send(q[6], pair)
    a1 = send(q[1], minus)
    e1 = send(add(q[5], g1).astype(BF), plus)
    c1 = send(add(q[3], d1).astype(BF), pair)
    b1 = send(add(q[2], e1, f1).astype(BF), plus)
    return add(q[0], a1, c1, b1)


CTX = ("x+", "x-", "yl")
LINE = ("z+", "z-", "yw")


def gather_ctx(v):
    own = gather8(v, *CTX)
    return own + [send(u, "core") for u in own]


def scatter_ctx(partial):
    half = partial.shape[0] // 2
    rows = half // 8
    got = send(partial[half:], "core")
    q = add(partial[:half], got).astype(BF)
    return scatter8([q[j * rows : (j + 1) * rows] for j in range(8)], *CTX)


def times_last(left, right):
    return lax.dot_general(left, right, (((1,), (1,)), ((), ())), preferred_element_type=F32)


def times_first(left, right):
    return lax.dot_general(left, right, (((0,), (0,)), ((), ())), preferred_element_type=F32)


def dot(left, right):
    return jnp.dot(left, right, preferred_element_type=F32)


def call(kernel, out_shape, n_in, **kw):
    return pl.pallas_call(
        kernel,
        out_shape=out_shape,
        in_specs=[pl.BlockSpec(memory_space=pltpu.SMEM)] + [pl.BlockSpec(memory_space=pltpu.VMEM)] * n_in,
        compiler_params=pltpu.CompilerParams(vmem_limit_bytes=VMEM_BYTES),
        **kw,
    )


def place_kernel(order, *refs):
    *parts, out = refs
    rows = parts[0].shape[0]
    for j, part in enumerate(parts):
        out[pl.ds(pl.multiple_of(order[j] * rows, 16), rows), :] = part[...]


def place(order, parts):
    rows, cols = parts[0].shape
    return call(place_kernel, jax.ShapeDtypeStruct((rows * len(parts), cols), parts[0].dtype), len(parts))(order, *parts)


def rotated(y, cosine, sine):
    return y * cosine + pltpu.roll(y, HEAD // 2, 1) * sine


def fwd_kernel(meta, *refs):
    xs = refs[:16]
    w, bias, cosine, sine, out, wide, q, k, v, lse = refs[16:]
    cut_one, cut_two = meta[16], meta[17]

    @pl.when(meta[18] == 1)
    def _():
        for r in range(16):
            here = pl.ds(pl.multiple_of(meta[r] * TOK, TOK), TOK)
            y = dot(xs[r][...], w[...]) + bias[...]
            cos_rows, sin_rows = cosine[here, :], sine[here, :]
            q[here, :] = rotated(y[:, :HEAD], cos_rows, sin_rows).astype(BF)
            k[here, :] = rotated(y[:, HEAD : 2 * HEAD], cos_rows, sin_rows).astype(BF)
            v[here, :] = y[:, 2 * HEAD :].astype(BF)
        for qb in range(SEQ // BQ):
            row = qb * BQ
            mine = q[row : row + BQ, :]
            places = row + lax.broadcasted_iota(jnp.int32, (BQ, 1), 0)
            begins = jnp.where(places < cut_one, 0, jnp.where(places < cut_two, cut_one, cut_two))
            first = jnp.where(row < cut_one, 0, jnp.where(row < cut_two, cut_one, cut_two))

            def step(kb, carry):
                top, total, acc = carry
                there = pl.ds(pl.multiple_of(kb * BK, BK), BK)
                s = times_last(mine, k[there, :]) * SCALE
                keys = kb * BK + lax.broadcasted_iota(jnp.int32, (1, BK), 1)
                s = jnp.where((keys <= places) & (keys >= begins), s, NEG)
                new = jnp.maximum(top, jnp.max(s, axis=1, keepdims=True))
                p = jnp.exp(s - new)
                fade = jnp.exp(top - new)
                total = total * fade + jnp.sum(p, axis=1, keepdims=True)
                acc = acc * fade + dot(p.astype(BF), v[there, :])
                return new, total, acc

            top, total, acc = lax.fori_loop(
                first // BK,
                row // BK + 1,
                step,
                (jnp.full((BQ, 1), NEG, F32), jnp.zeros((BQ, 1), F32), jnp.zeros((BQ, HEAD), F32)),
            )
            result = acc / total
            out[row : row + BQ, :] = result.astype(BF)
            wide[row : row + BQ, :] = result
            lse[row : row + BQ, :] = jnp.broadcast_to(top + jnp.log(total), (BQ, HEAD))


def bwd_kernel(meta, q, k, v, wide, lse, cosine, sine, grad, out, dq, dk, dv):
    cut_one, cut_two = meta[16], meta[17]

    @pl.when(meta[18] == 0)
    def _():
        out[...] = jnp.zeros_like(out)

    @pl.when(meta[18] == 1)
    def _():
        dk[...] = jnp.zeros_like(dk)
        dv[...] = jnp.zeros_like(dv)
        for qb in range(SEQ // BQ):
            row = qb * BQ
            mine = q[row : row + BQ, :]
            go = grad[row : row + BQ, :]
            log_sum = lse[row : row + BQ, :1]
            delta = jnp.sum(go.astype(F32) * wide[row : row + BQ, :], axis=1, keepdims=True)
            places = row + lax.broadcasted_iota(jnp.int32, (BQ, 1), 0)
            begins = jnp.where(places < cut_one, 0, jnp.where(places < cut_two, cut_one, cut_two))
            first = jnp.where(row < cut_one, 0, jnp.where(row < cut_two, cut_one, cut_two))

            def step(kb, acc):
                there = pl.ds(pl.multiple_of(kb * BK, BK), BK)
                keys_here = k[there, :]
                s = times_last(mine, keys_here) * SCALE
                keys = kb * BK + lax.broadcasted_iota(jnp.int32, (1, BK), 1)
                s = jnp.where((keys <= places) & (keys >= begins), s, NEG)
                p = jnp.exp(s - log_sum)
                dp = times_last(go, v[there, :])
                ds = (p * (dp - delta)).astype(BF)
                dv[there, :] += times_first(p.astype(BF), go)
                dk[there, :] += times_first(ds, mine)
                return acc + dot(ds, keys_here)

            dq[row : row + BQ, :] = lax.fori_loop(
                first // BK, row // BK + 1, step, jnp.zeros((BQ, HEAD), F32)
            )
        for r in range(16):
            here = pl.ds(pl.multiple_of(meta[r] * TOK, TOK), TOK)
            cos_rows, sin_rows = cosine[here, :], -sine[here, :]
            rows = slice(r * TOK, (r + 1) * TOK)
            out[rows, :HEAD] = rotated(dq[here, :] * SCALE, cos_rows, sin_rows).astype(BF)
            out[rows, HEAD : 2 * HEAD] = rotated(dk[here, :] * SCALE, cos_rows, sin_rows).astype(BF)
            out[rows, 2 * HEAD :] = dv[here, :].astype(BF)


def gate_up_kernel(slots, *refs):
    parts = refs[:16]
    gate, up, gain, held = refs[16:]
    for r in range(16):
        held[r] = parts[r][...]
    total = jnp.zeros((gain.shape[0], HEAD), F32)
    for s in range(16):
        block = held[slots[s]]
        gate[:, s * SLICE : (s + 1) * SLICE] = block[:, :SLICE].astype(F32)
        up[:, s * SLICE : (s + 1) * SLICE] = block[:, SLOT : SLOT + SLICE].astype(F32)
        total += block[:, SLOT - HEAD : SLOT].astype(F32)
    gain[...] = total


def gate_up_out(slots, parts):
    step = 32
    rows = parts[0].shape[0]
    return pl.pallas_call(
        gate_up_kernel,
        grid_spec=pltpu.PrefetchScalarGridSpec(
            num_scalar_prefetch=1,
            grid=(rows // step,),
            in_specs=[pl.BlockSpec((step, 2 * SLOT), lambda i, s: (i, 0))] * 16,
            out_specs=[
                pl.BlockSpec((step, FF), lambda i, s: (i, 0)),
                pl.BlockSpec((step, FF), lambda i, s: (i, 0)),
                pl.BlockSpec((step, HEAD), lambda i, s: (i, 0)),
            ],
            scratch_shapes=[pltpu.VMEM((16, step, 2 * SLOT), BF)],
        ),
        out_shape=[
            jax.ShapeDtypeStruct((rows, FF), F32),
            jax.ShapeDtypeStruct((rows, FF), F32),
            jax.ShapeDtypeStruct((rows, HEAD), F32),
        ],
        compiler_params=pltpu.CompilerParams(vmem_limit_bytes=VMEM_BYTES),
    )(slots, *parts)


def down_kernel(pieces, *refs):
    parts, out = refs[:16], refs[16]
    for r in range(16):
        half, piece = pieces[r] // 8, pieces[r] % 8

        @pl.when(piece < 7)
        def _():
            out[pl.ds(pl.multiple_of(half * SLICE + piece * PIECE, 16), PIECE), :] = parts[r][...].astype(F32)


def down_out(pieces, parts):
    step = 256
    return pl.pallas_call(
        down_kernel,
        grid_spec=pltpu.PrefetchScalarGridSpec(
            num_scalar_prefetch=1,
            grid=(D // step,),
            in_specs=[pl.BlockSpec((PIECE, step), lambda i, s: (0, i))] * 16,
            out_specs=pl.BlockSpec((2 * SLICE, step), lambda i, s: (0, i)),
        ),
        out_shape=jax.ShapeDtypeStruct((2 * SLICE, D), F32),
        compiler_params=pltpu.CompilerParams(vmem_limit_bytes=VMEM_BYTES),
    )(pieces, *parts)


def attn_kernel(slots, *refs):
    parts = refs[:16]
    wq, wk, wv, wo, aux, held = refs[16:]
    for r in range(16):
        held[r] = parts[r][...]
    for g in range(KV_HEADS):
        total = jnp.zeros((ROWS, 2 * HEAD), F32)
        for h in range(g * 6, g * 6 + 6):
            block = held[slots[h]].astype(F32)
            cols = slice(h * HEAD, (h + 1) * HEAD)
            wq[:, cols] = block[:ROWS, :HEAD]
            wo[:, cols] = block[:ROWS, 3 * HEAD :]
            total += block[:ROWS, HEAD : 3 * HEAD]
            aux[h] = block[ROWS:, :]
        wk[:, g * HEAD : (g + 1) * HEAD] = total[:, :HEAD]
        wv[:, g * HEAD : (g + 1) * HEAD] = total[:, HEAD:]


def attn_out(slots, parts):
    sds = jax.ShapeDtypeStruct
    return call(
        attn_kernel,
        [
            sds((ROWS, D), F32),
            sds((ROWS, 256), F32),
            sds((ROWS, 256), F32),
            sds((ROWS, D), F32),
            sds((HEADS, 16, 4 * HEAD), F32),
        ],
        16,
        scratch_shapes=[pltpu.VMEM((16, ROWS + 16, 4 * HEAD), BF)],
    )(slots, *parts)


def on_device(
    inputs,
    segments,
    gain_attn,
    w_query,
    b_query,
    w_key,
    b_key,
    w_value,
    b_value,
    w_output,
    gain_mlp,
    w_gate,
    w_up,
    w_down,
    cotangent,
):
    c, f = lax.axis_index("context"), lax.axis_index("fsdp")
    x, yl, core, z, yh = split_place(c, f)
    flip = 2 * yh
    s = c ^ flip
    head = jnp.minimum(s, HEADS - 1)
    group = head // (HEADS // KV_HEADS)
    rel_ctx = jnp.stack([((x + a) % 4) * 4 + (yl ^ b) * 2 + (core ^ k) for k in range(2) for a, b in REL8])
    rel_line = [((z + a) % 4) * 2 + (yh ^ b) for a, b in REL8]
    line_order = jnp.stack(rel_line).astype(jnp.int32)

    tokens = inputs[0].astype(F32)
    scale_one = lax.rsqrt(jnp.mean(tokens * tokens, axis=-1, keepdims=True) + EPS)
    unit_one = tokens * scale_one
    ones = gather_ctx(unit_one.astype(BF))

    own_ids = segments[0]
    cuts = lax.psum(
        jnp.stack([jnp.sum((own_ids < 1).astype(jnp.int32)), jnp.sum((own_ids < 2).astype(jnp.int32))]), "context"
    )
    places = jnp.arange(SEQ, dtype=jnp.int32)
    begins = jnp.where(places < cuts[0], 0, jnp.where(places < cuts[1], cuts[0], cuts[1]))
    freqs = THETA ** (-(jnp.arange(HEAD // 2, dtype=F32) * 2.0 / HEAD))
    angle = (places - begins).astype(F32)[:, None] * jnp.concatenate([freqs, freqs])[None, :]
    cosine = jnp.cos(angle)
    sine = jnp.sin(angle) * jnp.where(jnp.arange(HEAD) < HEAD // 2, -1.0, 1.0)[None, :]

    gain_one = gain_attn.astype(F32)[:, None]
    gain_two = gain_mlp.astype(F32)[:, None]
    wq_own = lax.dynamic_slice(w_query, (0, head * HEAD), (ROWS, HEAD))
    wk_own = lax.dynamic_slice(w_key, (0, group * HEAD), (ROWS, HEAD))
    wv_own = lax.dynamic_slice(w_value, (0, group * HEAD), (ROWS, HEAD))
    qkv_own = jnp.concatenate([wq_own, wk_own, wv_own], axis=1).astype(F32)
    bias_row = jnp.concatenate([b_query, b_key, b_value, jnp.zeros((128,), BF)])[None, :]
    piece = jnp.concatenate([(qkv_own * gain_one).astype(BF), jnp.pad(bias_row, ((0, 15), (0, 0)))], axis=0)
    attn_parts = place(line_order, gather8(piece, *LINE)).reshape(NFS, ROWS + 16, 3 * HEAD)
    w_qkv = attn_parts[:, :ROWS, :].reshape(D, 3 * HEAD)
    biases = attn_parts[:, ROWS, :].astype(F32)
    bias = jnp.concatenate(
        [
            lax.dynamic_slice(biases[:, :ROWS].reshape(D), (head * HEAD,), (HEAD,)),
            lax.dynamic_slice(biases[:, ROWS : ROWS + 32].reshape(256), (group * HEAD,), (HEAD,)),
            lax.dynamic_slice(biases[:, ROWS + 32 : ROWS + 64].reshape(256), (group * HEAD,), (HEAD,)),
        ]
    )[None, :]

    wo_mine = place(line_order, gather8(lax.dynamic_slice(w_output, (0, core * (D // 2)), (ROWS, D // 2)), *LINE))
    wo_other = send(wo_mine, "core")

    gate_own = lax.dynamic_slice(w_gate, (0, s * SLICE), (ROWS, SLICE))
    up_own = lax.dynamic_slice(w_up, (0, s * SLICE), (ROWS, SLICE))
    pad = ((0, 0), (0, SLOT - SLICE))
    gu_own = jnp.concatenate([jnp.pad(gate_own, pad), jnp.pad(up_own, pad)], axis=1).astype(F32)
    w_gu = place(line_order, gather8((gu_own * gain_two).astype(BF), *LINE))

    down_half, down_piece = c // 8, c % 8
    wd_own = lax.dynamic_slice(
        w_down, (down_half * SLICE + jnp.minimum(down_piece, 6) * PIECE, 0), (PIECE, D)
    ) * (down_piece < 7).astype(BF)
    w_d = place(line_order, gather8(send(wd_own, FROM_OWNER), *LINE))

    meta = jnp.concatenate([rel_ctx, cuts, (s < HEADS).astype(jnp.int32)[None]]).astype(jnp.int32)
    sds = jax.ShapeDtypeStruct
    att, wide, q, k, v, lse = call(
        fwd_kernel,
        [
            sds((SEQ, HEAD), BF),
            sds((SEQ, HEAD), F32),
            sds((SEQ, HEAD), BF),
            sds((SEQ, HEAD), BF),
            sds((SEQ, HEAD), BF),
            sds((SEQ, HEAD), F32),
        ],
        20,
    )(meta, *ones, w_qkv, bias, cosine, sine)

    def by_slice(blocks):
        pairs = blocks.reshape(*blocks.shape[:-2], 4, 2, 2, blocks.shape[-1])
        return jnp.where(yh == 1, pairs[..., ::-1, :, :], pairs).reshape(blocks.shape)

    attended = lax.all_to_all(att, "context", 0, 1, tiled=True)
    attended = by_slice(attended.reshape(TOK, NCTX, HEAD)).reshape(TOK, NCTX * HEAD)[:, :D]
    all_att = lax.all_gather(att, "context", axis=0)

    first, second = dot(attended, wo_mine), dot(attended, wo_other)
    mixed = jnp.where(core == 0, jnp.concatenate([first, second], 1), jnp.concatenate([second, first], 1))
    residual = tokens + mixed
    scale_two = lax.rsqrt(jnp.mean(residual * residual, axis=-1, keepdims=True) + EPS)
    unit_two = residual * scale_two

    u2 = jnp.concatenate(gather_ctx(unit_two.astype(BF)), axis=0)
    cot = jnp.concatenate(gather_ctx(cotangent[0]), axis=0)
    grad_hidden = times_last(cot, w_d)
    gate_up = dot(u2, w_gu)
    gate, upward = gate_up[:, :SLOT], gate_up[:, SLOT:]
    sig = jax.nn.sigmoid(gate)
    swished = gate * sig
    hidden = (swished * upward).astype(BF)
    grad_gate = grad_hidden * upward * sig * (1.0 + gate * (1.0 - sig))
    grad_up = grad_hidden * swished
    grad_gu = jnp.concatenate([grad_gate.astype(BF), grad_up.astype(BF)], axis=1)
    grad_unit_two = scatter_ctx(times_last(grad_gu, w_gu).astype(BF))
    down = scatter_ctx(dot(hidden, w_d).astype(BF))
    output = (residual + down).astype(BF)

    def line_parts(whole, rows):
        return [lax.dynamic_slice_in_dim(whole, at * rows, rows, 0) for at in rel_line]

    g_d = scatter8(line_parts(times_first(hidden, cot).astype(BF), PIECE), *LINE).astype(BF)
    down_pieces = gather_ctx(send(g_d, TO_OWNER))
    g_gu = scatter8(line_parts(times_first(u2, grad_gu).astype(BF), ROWS), *LINE)
    rowsum = jnp.sum(g_gu * gu_own, axis=1, keepdims=True)
    lane = jnp.arange(2 * SLOT, dtype=jnp.int32)[None, :]
    g_gu = jnp.where(lane == SLOT - 1, rowsum, g_gu * gain_two).astype(BF)
    gu_parts = gather_ctx(g_gu)

    grad_residual = cotangent[0].astype(F32) + scale_two * (
        grad_unit_two - unit_two * jnp.mean(grad_unit_two * unit_two, axis=-1, keepdims=True)
    )
    gao = grad_residual.astype(BF)
    gao_mine = jnp.where(core == 0, gao[:, : D // 2], gao[:, D // 2 :])
    gao_other = jnp.where(core == 0, gao[:, D // 2 :], gao[:, : D // 2])
    grad_att = (times_last(gao_mine, wo_mine) + times_last(gao_other, wo_other)).astype(BF)
    both = jnp.concatenate([grad_att.reshape(TOK, HEADS, HEAD), gao.reshape(TOK, HEADS, HEAD)], axis=2)
    both = jnp.pad(both, ((0, 0), (0, NCTX - HEADS), (0, 0)))
    both = by_slice(both).reshape(TOK, NCTX * 2 * HEAD)
    both = lax.all_to_all(both, "context", 1, 0, tiled=True)
    ga_head, gao_head = both[:, :HEAD], both[:, HEAD:]
    d_qkv = call(
        bwd_kernel,
        sds((SEQ, 3 * HEAD), BF),
        8,
        scratch_shapes=[pltpu.VMEM((SEQ, HEAD), F32)] * 3,
    )(meta, q, k, v, wide, lse, cosine, sine, ga_head)

    grad_unit_one = scatter_ctx(times_last(d_qkv, w_qkv).astype(BF))
    grad_tokens = grad_residual + scale_one * (
        grad_unit_one - unit_one * jnp.mean(grad_unit_one * unit_one, axis=-1, keepdims=True)
    )

    u1 = jnp.concatenate(ones, axis=0)
    dw_qkv = times_first(u1, d_qkv)
    dw_out = jnp.einsum("ctk,tm->ckm", all_att, gao_head, preferred_element_type=F32)
    dw_out = by_slice(dw_out.reshape(NCTX, HEAD * HEAD)).reshape(NCTX * HEAD, HEAD)[:D]
    dw_attn = jnp.concatenate([dw_qkv, dw_out], axis=1).astype(BF)
    bias_sums = jnp.sum(d_qkv.astype(F32), axis=0)
    bias_rows = jnp.pad(bias_sums[None, :], ((0, 15), (0, HEAD))).astype(BF)
    g_attn = scatter8(
        [jnp.concatenate([part, bias_rows], axis=0) for part in line_parts(dw_attn, ROWS)], *LINE
    )
    rowsum = jnp.sum(g_attn[:ROWS, : 3 * HEAD] * qkv_own, axis=1)
    scaled = jnp.concatenate([g_attn[:ROWS, : 3 * HEAD] * gain_one, g_attn[:ROWS, 3 * HEAD :]], axis=1)
    tail = jnp.concatenate(
        [g_attn[ROWS : ROWS + 1], jnp.pad(rowsum, (0, 4 * HEAD - ROWS))[None], jnp.zeros((14, 4 * HEAD), F32)], axis=0
    )
    attn_parts = gather_ctx(jnp.concatenate([scaled, tail], axis=0).astype(BF))

    def rel_of(places_wanted):
        dx = (places_wanted // 4 - x) % 4
        dy = ((places_wanted // 2) % 2) ^ yl
        key = dx * 2 + dy
        found = sum(
            jnp.where(key == ((a % 4) * 2 + b), j, 0) for j, (a, b) in enumerate(REL8)
        )
        return (found + 8 * ((places_wanted % 2) ^ core)).astype(jnp.int32)

    slots = rel_of(jnp.arange(NCTX, dtype=jnp.int32) ^ flip)
    grad_gate_w, grad_up_w, gain_two_cols = gate_up_out(slots, gu_parts)
    grad_gain_two = gain_two_cols[:, HEAD - 1]
    grad_down_w = down_out(rel_ctx.astype(jnp.int32), down_pieces)
    grad_wq, grad_wk, grad_wv, grad_wo, aux = attn_out(slots, attn_parts)
    sum_bq = lax.dynamic_slice(aux[:, 0, :HEAD].reshape(D), (f * ROWS,), (ROWS,))
    kv_sums = aux[:, 0, HEAD : 3 * HEAD].reshape(KV_HEADS, HEADS // KV_HEADS, 2 * HEAD).sum(axis=1)
    sum_bk = lax.dynamic_slice(kv_sums[:, :HEAD].reshape(256), (f * 32,), (32,))
    sum_bv = lax.dynamic_slice(kv_sums[:, HEAD:].reshape(256), (f * 32,), (32,))
    grad_gain_one = aux[:, 1, :ROWS].sum(axis=0)
    return (
        output[None],
        grad_tokens.astype(BF)[None],
        grad_gain_one,
        grad_wq,
        sum_bq,
        grad_wk,
        sum_bk,
        grad_wv,
        sum_bv,
        grad_wo,
        grad_gain_two,
        grad_gate_w,
        grad_up_w,
        grad_down_w,
    )


def solution(mesh):
    tokens = P("fsdp", "context", None)
    matrix, vector = P("fsdp", None), P("fsdp")
    return jax.shard_map(
        on_device,
        mesh=mesh,
        in_specs=(
            tokens,
            P("fsdp", "context"),
            vector,
            matrix,
            vector,
            matrix,
            vector,
            matrix,
            vector,
            matrix,
            vector,
            matrix,
            matrix,
            matrix,
            tokens,
        ),
        out_specs=(
            tokens,
            tokens,
            vector,
            matrix,
            vector,
            matrix,
            vector,
            matrix,
            vector,
            matrix,
            vector,
            matrix,
            matrix,
            matrix,
        ),
        check_vma=False,
    )
```

```python
import math

import jax
import jax.numpy as jnp
import numpy as np
from jax import lax
from jax.experimental import pallas as pl
from jax.experimental.pallas import tpu as pltpu
from jax.sharding import PartitionSpec as P

D = 1536
FF = 8960
HEADS = 12
KV_HEADS = 2
HEAD = 128
GROUP = HEADS // KV_HEADS
HALF = D // 2
PART = HALF + 2 * HEAD
SEQ = 2048
EPS = 1e-06
THETA = 1000000.0
NCTX, NFS = 16, 8
TOK = SEQ // NCTX
ROWS = D // NFS
BLOCK = FF // NFS // NCTX
PIECE = 80
SLOT = NFS * PIECE
SEND_ROWS = ROWS + PIECE + 16
AXES = ("context", "fsdp")
SCALE = 1.0 / math.sqrt(HEAD)
CHIP = 256
BK = 512
BF, F32 = jnp.bfloat16, jnp.float32
VMEM_BYTES = 58 * 1024 * 1024
NEG = -1e30


def split_place(c, f):
    return c // 4, (c // 2) % 2, c % 2, f // 2, f % 2


def pairs_of(move):
    pairs = []
    for c in range(NCTX):
        for f in range(NFS):
            x, yl, core, z, yh = move(*split_place(c, f))
            pairs.append((c * NFS + f, ((x % 4) * 4 + (yl % 2) * 2 + core % 2) * NFS + (z % 4) * 2 + yh % 2))
    return pairs


MOVES = {
    "x+": pairs_of(lambda x, yl, core, z, yh: (x + 1, yl, core, z, yh)),
    "x-": pairs_of(lambda x, yl, core, z, yh: (x - 1, yl, core, z, yh)),
    "yl": pairs_of(lambda x, yl, core, z, yh: (x, yl + 1, core, z, yh)),
    "core": pairs_of(lambda x, yl, core, z, yh: (x, yl, core + 1, z, yh)),
    "z+": pairs_of(lambda x, yl, core, z, yh: (x, yl, core, z + 1, yh)),
    "z-": pairs_of(lambda x, yl, core, z, yh: (x, yl, core, z - 1, yh)),
    "yw": pairs_of(lambda x, yl, core, z, yh: (x, yl + 1, core, z, yh + 1)),
}
SAME_CORE = [[c for c in range(NCTX) if c % 2 == core] for core in range(2)]


def send(value, move):
    pairs = MOVES[move] if isinstance(move, str) else move
    return lax.ppermute(value, AXES, pairs)


def add(*terms):
    total = terms[0].astype(F32)
    for t in terms[1:]:
        total = total + t.astype(F32)
    return total


def after(value, *earlier):
    return lax.optimization_barrier((value, *earlier))[0]


def together(sends, *rest):
    got = [send(value, move) for value, move in sends]
    done = lax.optimization_barrier((*got, *rest))
    return list(done[: len(got)]), list(done[len(got) :])


REL8 = [(0, 0), (-1, 0), (1, 0), (0, 1), (-1, 1), (2, 0), (1, 1), (2, 1)]
CTX, SLICES = ("x+", "x-", "yl"), ("z+", "z-", "yw")


def over_chips(terms):
    return lax.all_to_all(terms, "context", 0, 0, axis_index_groups=SAME_CORE, tiled=True)


def gather_one(v, way):
    return [(v, way[0]), (v, way[1]), (v, way[2])]


def gather_two(parts, way):
    _, b, c = parts
    return [(c, way[0]), (b, way[1]), (b, way[2])]


def gather_three(parts, way):
    return [(parts[1], way[2])]


def sum_one(q, way):
    return [(q(7), way[2]), (q(4), way[1])]


def sum_two(q, got, way):
    return [(add(q(5), got[0]).astype(BF), way[0]), (q(6), way[2]), (q(1), way[1])]


def sum_three(q, one, two, way):
    return [(add(q(2), two[0], two[1]).astype(BF), way[0]), (add(q(3), one[1]).astype(BF), way[2])]


def sum_all(q, two, three):
    return add(q(0), two[2], three[0], three[1])


def pair_sum(mine, other):
    n = mine.shape[0] // 8
    return lambda j: add(mine[j * n : (j + 1) * n], other[j * n : (j + 1) * n]).astype(BF)


def times_last(left, right):
    return lax.dot_general(left, right, (((1,), (1,)), ((), ())), preferred_element_type=F32)


def times_first(left, right):
    return lax.dot_general(left, right, (((0,), (0,)), ((), ())), preferred_element_type=F32)


def dot(left, right):
    return jnp.dot(left, right, preferred_element_type=F32)


def sds(shape, dtype=BF):
    return jax.ShapeDtypeStruct(shape, dtype)


WHOLE = pl.BlockSpec(memory_space=pltpu.VMEM)
SCALARS = pl.BlockSpec(memory_space=pltpu.SMEM)
ANYWHERE = pl.BlockSpec(memory_space=pl.ANY)


def call(kernel, out_shape, specs, us, **kw):
    return pl.pallas_call(
        kernel,
        out_shape=out_shape,
        in_specs=specs,
        compiler_params=pltpu.CompilerParams(vmem_limit_bytes=VMEM_BYTES),
        cost_estimate=pl.CostEstimate(flops=int(us * 1.0e9), bytes_accessed=int(us * 1e5), transcendentals=0),
        **kw,
    )


def first_kernel(
    at, tokens, ids, w_query, w_key, w_value, w_out, gain, b_query, b_key, b_value, unit, piece, wide, narrow
):
    f, core = at[0], at[1]
    x = tokens[...].astype(F32)
    unit[:TOK, :] = (x * lax.rsqrt(jnp.mean(x * x, axis=1, keepdims=True) + EPS)).astype(BF)
    lane = lax.broadcasted_iota(jnp.int32, (16, D), 1)
    before = [jnp.sum((ids[...] < n).astype(F32), axis=1, keepdims=True) for n in (1, 2)]
    unit[TOK:, :] = jnp.where(lane == 0, before[0], jnp.where(lane == 1, before[1], 0.0)).astype(BF)
    scale = gain[...]
    qs = pl.ds(pl.multiple_of(core * HALF, HALF), HALF)
    ks = pl.ds(pl.multiple_of(core * HEAD, HEAD), HEAD)
    piece[:ROWS, :HALF] = (w_query[:, qs].astype(F32) * scale).astype(BF)
    piece[:ROWS, HALF : HALF + HEAD] = (w_key[:, ks].astype(F32) * scale).astype(BF)
    piece[:ROWS, PART:] = w_out[:, qs]
    piece[:ROWS, HALF + HEAD : PART] = (w_value[:, ks].astype(F32) * scale).astype(BF)
    piece[ROWS:, :] = jnp.zeros((16, PART + HALF), BF)
    wide[...] = jnp.zeros_like(wide)
    wide[0:1, :ROWS] = b_query[...]
    wide[...] = pltpu.roll(wide[...], f * ROWS, 1)
    piece[ROWS : ROWS + 8, :HALF] = wide[:, qs].astype(BF)
    for b, at_col in ((b_key, HALF), (b_value, HALF + HEAD)):
        narrow[...] = jnp.zeros_like(narrow)
        narrow[0:1, :32] = b[...]
        narrow[...] = pltpu.roll(narrow[...], f * 32, 1)
        piece[ROWS : ROWS + 8, at_col : at_col + HEAD] = narrow[:, ks].astype(BF)


def both_cores(core, mine, theirs, out):
    n = mine.shape[0]
    out[pl.ds(pl.multiple_of(core * n, n), n), :] = mine
    out[pl.ds(pl.multiple_of((1 - core) * n, n), n), :] = theirs


def rotated(y, cosine, sine):
    return y * cosine + pltpu.roll(y, HEAD // 2, 1) * sine


def project_kernel(meta, unit, unit_other, *refs):
    parts, (cosine, sine, q, kv, w, units) = refs[:8], refs[8:]
    core, chip = meta[0], meta[1]
    both_cores(core, unit[:TOK, :], unit_other[:TOK, :], units)
    bias = jnp.zeros((1, PART), F32)
    for j in range(8):
        w[pl.ds(pl.multiple_of(meta[2 + j] * ROWS, ROWS), ROWS), :] = parts[j][:ROWS, :PART]
        bias += parts[j][ROWS:, :PART].astype(F32)[:1]
    y = dot(units[...], w[...]) + bias
    here = pl.ds(pl.multiple_of(chip * CHIP, CHIP), CHIP)
    cos_rows, sin_rows = cosine[here, :], sine[here, :]
    for h in range(GROUP):
        q[h * CHIP : (h + 1) * CHIP, :] = rotated(y[:, h * HEAD : (h + 1) * HEAD], cos_rows, sin_rows).astype(BF)
    kv[:CHIP, :HEAD] = rotated(y[:, HALF : HALF + HEAD], cos_rows, sin_rows).astype(BF)
    kv[:CHIP, HEAD:] = y[:, HALF + HEAD :].astype(BF)
    counts = unit[TOK:, : 2 * HEAD].astype(F32) + unit_other[TOK:, : 2 * HEAD].astype(F32)
    kv[CHIP:, :] = counts.astype(BF)


def doc_begins(cuts, places):
    return jnp.where(places < cuts[0], 0, jnp.where(places < cuts[1], cuts[0], cuts[1]))


def visible_keys(cuts, chip, kb):
    places = chip * CHIP + lax.broadcasted_iota(jnp.int32, (CHIP, 1), 0)
    keys = kb * BK + lax.broadcasted_iota(jnp.int32, (1, BK), 1)
    return (keys <= places) & (keys >= doc_begins(cuts, places))


def key_blocks(cuts, chip):
    return doc_begins(cuts, chip * CHIP) // BK, chip // (BK // CHIP) + 1


def fwd_kernel(meta, q, *refs):
    parts, out, wide, lse, k, v, cuts_out, top, total, acc = refs
    chip = meta[1]
    lane = lax.broadcasted_iota(jnp.int32, (1, HEAD), 1)
    counts = sum(parts[j, CHIP:, :HEAD].astype(F32) for j in range(8))[:1]
    cuts = [jnp.sum(jnp.where(lane == i, counts, 0.0)).astype(jnp.int32) for i in range(2)]
    cuts_out[0], cuts_out[1] = cuts
    for j in range(8):
        there = slice(j * CHIP, (j + 1) * CHIP)
        k[there, :] = parts[j, :CHIP, :HEAD]
        v[there, :] = parts[j, :CHIP, HEAD:]
    top[...] = jnp.full_like(top, NEG)
    total[...] = jnp.zeros_like(total)
    acc[...] = jnp.zeros_like(acc)

    def step(kb, _):
        there = pl.ds(pl.multiple_of(kb * BK, BK), BK)
        keys, vals = k[there, :], v[there, :]
        visible = visible_keys(cuts, chip, kb)
        for h in range(GROUP):
            rows = slice(h * CHIP, (h + 1) * CHIP)
            s = jnp.where(visible, times_last(q[rows, :], keys) * SCALE, NEG)
            old = top[rows, :]
            new = jnp.maximum(old, jnp.max(s, axis=1, keepdims=True))
            p = jnp.exp(s - new[:, :1])
            fade = jnp.exp(old - new)
            top[rows, :] = new
            total[rows, :] = total[rows, :] * fade + jnp.sum(p, axis=1, keepdims=True)
            acc[rows, :] = acc[rows, :] * fade + dot(p.astype(BF), vals)
        return 0

    lo, hi = key_blocks(cuts, chip)
    lax.fori_loop(lo, hi, step, 0)
    for h in range(GROUP):
        rows, cols = slice(h * CHIP, (h + 1) * CHIP), slice(h * HEAD, (h + 1) * HEAD)
        result = acc[rows, :] / total[rows, :]
        out[:, cols] = result.astype(BF)
        wide[rows, :] = result
        lse[rows, :] = top[rows, :] + jnp.log(total[rows, :])


def bwd_kernel(meta, cuts_in, q, k, v, wide, lse, cosine, sine, grad, grad_other, dq_out, dkv, go, delta, p_all, ds_all, dq, dk, dv):
    core, chip = meta[0], meta[1]
    cuts = (cuts_in[0], cuts_in[1])
    dq[...] = jnp.zeros_like(dq)
    dk[...] = jnp.zeros_like(dk)
    dv[...] = jnp.zeros_like(dv)
    for h in range(GROUP):
        rows, cols = slice(h * CHIP, (h + 1) * CHIP), slice(h * HEAD, (h + 1) * HEAD)
        low = (grad[:, cols] + grad_other[:, cols].astype(F32)).astype(BF)
        go[rows, :] = low
        found = jnp.sum(low.astype(F32) * wide[rows, :], axis=1, keepdims=True)
        delta[rows, :] = jnp.broadcast_to(found, (CHIP, HEAD))

    def step(kb, _):
        there = pl.ds(pl.multiple_of(kb * BK, BK), BK)
        keys, vals = k[there, :], v[there, :]
        visible = visible_keys(cuts, chip, kb)
        for h in range(GROUP):
            rows = slice(h * CHIP, (h + 1) * CHIP)
            s = jnp.where(visible, times_last(q[rows, :], keys) * SCALE, NEG)
            p = jnp.exp(s - lse[rows, :1])
            dp = times_last(go[rows, :], vals)
            ds = (p * (dp - delta[rows, :1])).astype(BF)
            p_all[rows, :] = p.astype(BF)
            ds_all[rows, :] = ds
            dq[rows, :] += dot(ds, keys)
        dv[there, :] = times_first(p_all[...], go[...])
        dk[there, :] = times_first(ds_all[...], q[...])
        return 0

    lo, hi = key_blocks(cuts, chip)
    lax.fori_loop(lo, hi, step, 0)
    here = pl.ds(pl.multiple_of(chip * CHIP, CHIP), CHIP)
    cos_rows, sin_rows = cosine[here, :], -sine[here, :]
    for h in range(GROUP):
        rows, cols = slice(h * CHIP, (h + 1) * CHIP), slice(h * HEAD, (h + 1) * HEAD)
        dq_out[:, cols] = rotated(dq[rows, :] * SCALE, cos_rows, sin_rows).astype(BF)
    dkv[:, :HEAD] = (dk[...] * SCALE).astype(BF)
    dkv[:, HEAD:] = dv[...].astype(BF)


def out_kernel(meta, att, att_other, *refs):
    parts, (mine, theirs, atts, w_turned, w, held) = refs[:8], refs[8:]
    core = meta[0]
    atts[:, pl.ds(pl.multiple_of(core * HALF, HALF), HALF)] = att[...]
    atts[:, pl.ds(pl.multiple_of((1 - core) * HALF, HALF), HALF)] = att_other[...]
    for j in range(8):
        w[pl.ds(pl.multiple_of(meta[2 + j] * ROWS, ROWS), ROWS), :] = parts[j][:ROWS, PART:]
    held[...] = dot(atts[...], w[...])
    mine[...] = held[pl.ds(pl.multiple_of(core * TOK, TOK), TOK), :]
    theirs[...] = held[pl.ds(pl.multiple_of((1 - core) * TOK, TOK), TOK), :]
    for i in range(HALF // 256):
        cols = slice(i * 256, (i + 1) * 256)
        w_turned[cols, :] = jnp.transpose(w[:, cols])


def residual_kernel(meta, tokens, mine, got, residual, unit):
    core = meta[0]
    here = pl.ds(pl.multiple_of(core * HALF, HALF), HALF)
    there = pl.ds(pl.multiple_of((1 - core) * HALF, HALF), HALF)
    residual[:, here] = tokens[:, here].astype(F32) + mine[...]
    residual[:, there] = tokens[:, there].astype(F32) + got[...]
    x = residual[...]
    unit[...] = (x * lax.rsqrt(jnp.mean(x * x, axis=1, keepdims=True) + EPS)).astype(BF)


def norm_grad(x, grad):
    scale = lax.rsqrt(jnp.mean(x * x, axis=1, keepdims=True) + EPS)
    unit = x * scale
    return scale * (grad - unit * jnp.mean(grad * unit, axis=1, keepdims=True))


def norm_two_kernel(meta, term, a, b, c, residual, cot, grad_residual, mine, theirs, held):
    core = meta[0]
    grad = add(term[...], a[...], b[...], c[...])
    result = cot[...].astype(F32) + norm_grad(residual[...], grad)
    grad_residual[...] = result
    held[...] = result.astype(BF)
    mine[...] = held[:, pl.ds(pl.multiple_of(core * HALF, HALF), HALF)]
    theirs[...] = held[:, pl.ds(pl.multiple_of((1 - core) * HALF, HALF), HALF)]


def out_grad_kernel(meta, grad, grad_other, w_turned, mine, theirs, grads, held):
    core = meta[0]
    both_cores(core, grad[...], grad_other[...], grads)
    held[...] = dot(grads[...], w_turned[...])
    mine[...] = held[:, pl.ds(pl.multiple_of(core * HALF, HALF), HALF)]
    theirs[...] = held[:, pl.ds(pl.multiple_of((1 - core) * HALF, HALF), HALF)].astype(BF)


def project_grad_kernel(meta, terms, dq, units, w_turned, cosine, sine, atts, grads, mine, theirs, *refs):
    pieces, (both, dw, held) = refs[:8], refs[8:]
    core, chip = meta[0], meta[1]
    here = pl.ds(pl.multiple_of(chip * CHIP, CHIP), CHIP)
    dkv = add(*[terms[j * CHIP : (j + 1) * CHIP, :] for j in range(8)])
    both[:, :HALF] = dq[...]
    both[:, HALF : HALF + HEAD] = rotated(dkv[:, :HEAD], cosine[here, :], -sine[here, :]).astype(BF)
    both[:, HALF + HEAD :] = dkv[:, HEAD:].astype(BF)
    held[...] = dot(both[...], w_turned[...])
    mine[...] = held[pl.ds(pl.multiple_of(core * TOK, TOK), TOK), :]
    theirs[...] = held[pl.ds(pl.multiple_of((1 - core) * TOK, TOK), TOK), :].astype(BF)
    dw[:, :PART] = times_first(units[...], both[...]).astype(BF)
    dw[:, PART:] = times_first(atts[...], grads[...]).astype(BF)
    bias = jnp.sum(both[...].astype(F32), axis=0, keepdims=True)
    bias = jnp.broadcast_to(bias, (16, PART)).astype(BF)
    for j, out in enumerate(pieces):
        out[:ROWS, :] = dw[pl.ds(pl.multiple_of(meta[2 + j] * ROWS, ROWS), ROWS), :]
        out[ROWS:, :PART] = bias
        out[ROWS:, PART:] = jnp.zeros((16, HALF), BF)


def norm_one_kernel(mine, got, tokens, grad_residual, out):
    grad = mine[...] + got[...].astype(F32)
    out[...] = (grad_residual[...] + norm_grad(tokens[...].astype(F32), grad)).astype(BF)


def line_deal_kernel(term, a, b, c, *refs):
    out, total = refs
    total[...] = add(term[...], a[...], b[...], c[...])
    for chip in range(8):
        out[chip, :, :HEAD] = total[:, chip * HEAD : (chip + 1) * HEAD].astype(BF)
        at = PART + min(chip, GROUP - 1) * HEAD
        out[chip, :, HEAD:] = total[:, at : at + HEAD].astype(BF)


def block_kernel(meta, terms, w_query, w_key, w_value, gain, out):
    core, chip = meta[0], meta[1]
    total = add(*[terms[j] for j in range(8)])
    head = core * GROUP + jnp.minimum(chip, GROUP - 1)
    wq = w_query[:, pl.ds(pl.multiple_of(head * HEAD, HEAD), HEAD)].astype(F32)
    ks = pl.ds(pl.multiple_of(core * HEAD, HEAD), HEAD)
    wk, wv = w_key[:, ks].astype(F32), w_value[:, ks].astype(F32)
    w = jnp.where(chip < GROUP, wq, jnp.where(chip == GROUP, wk, wv))
    grad = total[:ROWS, :HEAD]
    for_gain = jnp.sum(grad * w, axis=1, keepdims=True)
    for_gain = jnp.transpose(jnp.broadcast_to(for_gain, (ROWS, HEAD)))
    out[:ROWS, :HEAD] = (grad * gain[...]).astype(BF)
    out[:ROWS, HEAD:] = total[:ROWS, HEAD:].astype(BF)
    row = lax.broadcasted_iota(jnp.int32, (16, 2 * HEAD), 0)
    gains = jnp.concatenate([for_gain[:16, :], jnp.zeros((16, 2 * HEAD - ROWS), F32)], axis=1)
    out[ROWS:, :] = jnp.where(row == 0, total[ROWS:, :], gains).astype(BF)


def attn_kernel(slots, *refs):
    held, wq, wk, wv, wo, bq, bk, bv, gain, wide, narrow = refs[0:2], *refs[2:]
    f, mine = slots[0], slots[1]
    total = jnp.zeros((16, 2 * HEAD), F32)
    for core in range(2):
        cols = slice(core * HEAD, (core + 1) * HEAD)
        for chip in range(8):
            block = jnp.where(mine == core, held[0][chip], held[1][chip]).astype(F32)
            total += block[ROWS:, :]
            if chip < GROUP:
                at = slice((core * GROUP + chip) * HEAD, (core * GROUP + chip + 1) * HEAD)
                wq[:, at] = block[:ROWS, :HEAD]
                wo[:, at] = block[:ROWS, HEAD:]
                wide[:, at] = block[ROWS : ROWS + 8, :HEAD]
            else:
                out, i = ((wk, 0), (wv, 1))[chip - GROUP]
                out[:, cols] = block[:ROWS, :HEAD]
                narrow[i, :, cols] = block[ROWS : ROWS + 8, :HEAD]
    gain[...] = total[1:2, :ROWS]
    bq[...] = pltpu.roll(wide[...], D - f * ROWS, 1)[:1, :ROWS]
    bk[...] = pltpu.roll(narrow[0], 256 - f * 32, 1)[:1, :32]
    bv[...] = pltpu.roll(narrow[1], 256 - f * 32, 1)[:1, :32]


WIDE = 2 * SLOT
TAIL = D - WIDE


def slice_kernel(at, w_gate, w_up, w_down, gain, out, own, gathered):
    lane = lax.broadcasted_iota(jnp.int32, (ROWS, PIECE), 1)
    for i, w in enumerate((w_gate, w_up)):
        for j in range(NFS):
            start = j * (FF // NFS) + at[0] * BLOCK
            base = jnp.minimum(start // 128 * 128, FF - 256)
            window = w[:, pl.ds(pl.multiple_of(base, 128), 256)].astype(F32)
            window = pltpu.roll(window, 256 - (start - base), 1)[:, :PIECE]
            gathered[:, i * SLOT + j * PIECE : i * SLOT + (j + 1) * PIECE] = jnp.where(lane < BLOCK, window, 0.0)
    own[...] = gathered[...].astype(BF)
    out[:ROWS, :] = (gathered[...] * gain[...]).astype(BF)
    start = at[0] * BLOCK
    base = jnp.minimum(start // 16 * 16, FF // NFS - 96)
    window = w_down[pl.ds(pl.multiple_of(base, 16), 96), :].astype(F32)
    window = pltpu.roll(window, 96 - (start - base), 0)[:PIECE]
    row = lax.broadcasted_iota(jnp.int32, (PIECE, D), 0)
    put_down(out, jnp.where(row < BLOCK, window, 0.0).astype(BF))


def put_down(out, rows):
    out[ROWS : ROWS + PIECE, :] = rows[:, :WIDE]
    for i in range(PIECE // 16):
        out[ROWS + PIECE :, i * TAIL : (i + 1) * TAIL] = rows[i * 16 : (i + 1) * 16, WIDE:]


def take_down(part):
    tail = [part[ROWS + PIECE :, i * TAIL : (i + 1) * TAIL] for i in range(PIECE // 16)]
    return jnp.concatenate([part[ROWS : ROWS + PIECE, :], jnp.concatenate(tail, axis=0)], axis=1)


def weights_kernel(order, *refs):
    parts, qkv = refs[:8], refs[8]
    w, w_turned, down, qkv_turned = refs[9:]
    for j in range(8):
        w[pl.ds(pl.multiple_of(order[j] * ROWS, ROWS), ROWS), :WIDE] = parts[j][:ROWS, :]
        down[pl.ds(pl.multiple_of(order[j] * PIECE, 16), PIECE), :] = take_down(parts[j])
    for i in range(WIDE // 256):
        w_turned[i * 256 : (i + 1) * 256, :] = jnp.transpose(w[:, i * 256 : (i + 1) * 256])
    for i in range(SLOT // 128):
        w[:, WIDE + i * 128 : WIDE + (i + 1) * 128] = jnp.transpose(down[i * 128 : (i + 1) * 128, :])
    for i in range(PART // 256):
        qkv_turned[i * 256 : (i + 1) * 256, :] = jnp.transpose(qkv[:, i * 256 : (i + 1) * 256])


def deal_kernel(order, wide, down, *outs):
    for j, out in enumerate(outs):
        out[:ROWS, :] = wide[pl.ds(pl.multiple_of(order[j] * ROWS, ROWS), ROWS), :]
        put_down(out, down[pl.ds(pl.multiple_of(order[j] * PIECE, 16), PIECE), :])


def slice_sum_kernel(term, a, b, c, own, gain, out):
    total = add(term[...], a[...], b[...], c[...])
    grad = total[:ROWS, :]
    for_gain = jnp.sum(grad * own[...].astype(F32), axis=1, keepdims=True)
    lane = lax.broadcasted_iota(jnp.int32, (ROWS, WIDE), 1)
    out[:ROWS, :] = jnp.where(lane == SLOT - 1, for_gain, grad * gain[...]).astype(BF)
    out[ROWS:, :] = total[ROWS:, :].astype(BF)


MB = 256


def mlp_kernel(meta, *refs):
    us, (cots, w_in, w_turned_in) = refs[:16], refs[16:19]
    u_out, hidden_out, grad_out, mine_out, other_out = refs[19:24]
    u, c, hidden, grad, res, w, w_turned, in_sem, out_sem = refs[24:]

    def rows_of(i, n):
        return pl.ds(pl.multiple_of(i * n, n), n)

    loads = [
        pltpu.make_async_copy(w_in, w, in_sem.at[32]),
        pltpu.make_async_copy(w_turned_in, w_turned, in_sem.at[33]),
    ]
    for load in loads:
        load.start()
    for r in range(16):
        here = pl.ds(r * TOK, TOK)
        pltpu.make_async_copy(us[r], u.at[here, :], in_sem.at[r]).start()
        pltpu.make_async_copy(cots.at[rows_of(meta[r], TOK), :], c.at[here, :], in_sem.at[16 + r]).start()
    for load in loads:
        load.wait()

    def results(i):
        rows = rows_of(i, MB)
        return [
            pltpu.make_async_copy(u.at[rows, :], u_out.at[rows, :], out_sem.at[7 * i]),
            pltpu.make_async_copy(grad.at[rows, :], grad_out.at[rows, :], out_sem.at[7 * i + 1]),
        ] + [
            pltpu.make_async_copy(
                hidden.at[rows_of(2 * i + h, TOK), :],
                hidden_out.at[rows_of(meta[2 * i + h], TOK), :],
                out_sem.at[7 * i + 2 + h],
            )
            for h in range(2)
        ]

    def last(i, to):
        return pltpu.make_async_copy(res.at[rows_of(i, MB), :], to.at[rows_of(lax.rem(i, 4), MB), :], out_sem.at[7 * i + 4])

    def step(i, _):
        for h in range(2):
            rows = rows_of(2 * i + h, TOK)
            pltpu.make_async_copy(us[0], u.at[rows, :], in_sem.at[2 * i + h]).wait()
            pltpu.make_async_copy(us[0], c.at[rows, :], in_sem.at[16 + 2 * i + h]).wait()
        rows = rows_of(i, MB)
        x = u[rows, :]
        gate = dot(x, w[:, :SLOT])
        upward = dot(x, w[:, SLOT : 2 * SLOT])
        back = dot(c[rows, :], w[:, 2 * SLOT :])
        sig = jax.nn.sigmoid(gate)
        swished = gate * sig
        hidden[rows, :] = (swished * upward).astype(BF)
        grad[rows, :SLOT] = (back * upward * sig * (1.0 + gate * (1.0 - sig))).astype(BF)
        grad[rows, SLOT:] = (back * swished).astype(BF)
        for one in results(i):
            one.start()
        res[rows, :] = dot(grad[rows, :], w_turned[...]).astype(BF)

        @pl.when(i < 4)
        def _():
            last(i, mine_out).start()

        @pl.when(i >= 4)
        def _():
            last(i, other_out).start()

        return 0

    lax.fori_loop(0, SEQ // MB, step, 0)

    def finish(i, _):
        for one in results(i):
            one.wait()
        last(i, mine_out).wait()
        return 0

    lax.fori_loop(0, SEQ // MB, finish, 0)


def mlp(meta, us, cots, w, w_turned):
    return call(
        mlp_kernel,
        [sds((SEQ, D)), sds((SEQ, SLOT)), sds((SEQ, 2 * SLOT)), sds((SEQ // 2, D)), sds((SEQ // 2, D))],
        [SCALARS] + [ANYWHERE] * 19,
        25,
        out_specs=[ANYWHERE] * 5,
        scratch_shapes=[
            pltpu.VMEM((SEQ, D), BF),
            pltpu.VMEM((SEQ, D), BF),
            pltpu.VMEM((SEQ, SLOT), BF),
            pltpu.VMEM((SEQ, 2 * SLOT), BF),
            pltpu.VMEM((SEQ, D), BF),
            pltpu.VMEM((D, 3 * SLOT), BF),
            pltpu.VMEM((2 * SLOT, D), BF),
            pltpu.SemaphoreType.DMA((34,)),
            pltpu.SemaphoreType.DMA((56,)),
        ],
    )(meta, *us, cots, w, w_turned)


def through_down_kernel(order, hidden, w, mine, other):
    def step(i, _):
        rows = [hidden[pl.ds(pl.multiple_of(order[2 * i + h] * TOK, TOK), TOK), :] for h in range(2)]
        result = dot(jnp.concatenate(rows, axis=0), w[...]).astype(BF)
        there = pl.ds(pl.multiple_of(lax.rem(i, 4) * MB, MB), MB)

        @pl.when(i < 4)
        def _():
            mine[there, :] = result

        @pl.when(i >= 4)
        def _():
            other[there, :] = result

        return 0

    lax.fori_loop(0, SEQ // MB, step, 0)


def through_down(order, hidden, w):
    return call(through_down_kernel, [sds((SEQ // 2, D)), sds((SEQ // 2, D))], [SCALARS, WHOLE, WHOLE], 8)(
        order, hidden, w
    )


def gate_up_kernel(slots, parts, gate, up, gain):
    total = jnp.zeros((gain.shape[0], HEAD), F32)
    for s in range(16):
        block = parts[slots[s]]
        for i, out in enumerate((gate, up)):
            wide = block[:, i * SLOT : (i + 1) * SLOT].astype(F32)
            for j in range(NFS):
                at = j * (FF // NFS) + s * BLOCK
                out[:, at : at + BLOCK] = wide[:, j * PIECE : j * PIECE + BLOCK]
        total += block[:, SLOT - HEAD : SLOT].astype(F32)
    gain[...] = total


def gate_up_out(slots, parts):
    step = 32
    return pl.pallas_call(
        gate_up_kernel,
        grid_spec=pltpu.PrefetchScalarGridSpec(
            num_scalar_prefetch=1,
            grid=(ROWS // step,),
            in_specs=[pl.BlockSpec((NCTX, step, 2 * SLOT), lambda i, s: (0, i, 0))],
            out_specs=[
                pl.BlockSpec((step, FF), lambda i, s: (i, 0)),
                pl.BlockSpec((step, FF), lambda i, s: (i, 0)),
                pl.BlockSpec((step, HEAD), lambda i, s: (i, 0)),
            ],
        ),
        out_shape=[sds((ROWS, FF), F32), sds((ROWS, FF), F32), sds((ROWS, HEAD), F32)],
        compiler_params=pltpu.CompilerParams(vmem_limit_bytes=VMEM_BYTES),
        cost_estimate=pl.CostEstimate(flops=10000000000, bytes_accessed=1000000, transcendentals=0),
    )(slots, parts)


def down_kernel(slots, parts, out):
    for s in range(16):
        rows = take_down(parts.at[slots[s]]).astype(F32)
        out[s * BLOCK : (s + 1) * BLOCK, :] = rows[:BLOCK]


def down_out(slots, parts):
    return call(down_kernel, sds((FF // NFS, D), F32), [SCALARS, WHOLE], 8)(slots, parts)


def angle_tables():
    freqs = THETA ** (-(np.arange(HEAD // 2) * 2.0 / HEAD))
    angle = np.arange(SEQ)[:, None] * np.concatenate([freqs, freqs])[None, :]
    turn = np.where(np.arange(HEAD) < HEAD // 2, -1.0, 1.0)[None, :]
    return jnp.asarray(np.cos(angle), F32), jnp.asarray(np.sin(angle) * turn, F32)


def on_device(
    inputs,
    segments,
    gain_attn,
    w_query,
    b_query,
    w_key,
    b_key,
    w_value,
    b_value,
    w_output,
    gain_mlp,
    w_gate,
    w_up,
    w_down,
    cotangent,
):
    c, f = lax.axis_index("context"), lax.axis_index("fsdp")
    x, yl, core, z, yh = split_place(c, f)
    rel_ctx = jnp.stack([((x + a) % 4) * 4 + (yl ^ b) * 2 + (core ^ k) for k in range(2) for a, b in REL8])
    rel_ctx = rel_ctx.astype(jnp.int32)
    rel_shard = [((z + a) % 4) * 2 + (yh ^ b) for a, b in REL8]
    meta = jnp.stack([core, c // 2, *rel_shard]).astype(jnp.int32)
    rel_line = meta[2:10]
    cosine, sine = angle_tables()
    gain_one = gain_attn.astype(F32)[:, None]
    gain_two = gain_mlp.astype(F32)[:, None]
    tokens, cot = inputs[0], cotangent[0]

    unit, piece = call(
        first_kernel,
        [sds((TOK + 16, D)), sds((ROWS + 16, PART + HALF))],
        [SCALARS] + [WHOLE] * 10,
        3,
        scratch_shapes=[pltpu.VMEM((8, D), F32), pltpu.VMEM((8, 256), F32)],
    )(
        jnp.stack([f, core]).astype(jnp.int32),
        tokens,
        segments,
        w_query,
        w_key,
        w_value,
        w_output,
        gain_one,
        b_query.astype(F32)[None],
        b_key.astype(F32)[None],
        b_value.astype(F32)[None],
    )
    mlp_piece, gu_own = call(
        slice_kernel,
        [sds((SEND_ROWS, WIDE)), sds((ROWS, WIDE))],
        [SCALARS] + [WHOLE] * 4,
        6,
        scratch_shapes=[pltpu.VMEM((ROWS, WIDE), F32)],
    )((c ^ (2 * yh))[None].astype(jnp.int32), w_gate, w_up, w_down, gain_two)
    got, _ = together(gather_one(piece, SLICES) + [(unit, "core")])
    one, unit_other = got[:3], got[3]
    cots = lax.all_gather(after(cot, *got), "context", axis=0, tiled=True)
    two, (mlp_piece, gu_own) = together(gather_two(one, SLICES), mlp_piece, gu_own)
    three, _ = together(gather_three(two, SLICES))

    q, kv, w_part, units = call(
        project_kernel,
        [sds((GROUP * CHIP, HEAD)), sds((CHIP + 16, 2 * HEAD)), sds((D, PART)), sds((CHIP, D))],
        [SCALARS] + [WHOLE] * 12,
        5,
    )(meta, unit, unit_other, piece, *one, *two, *three, cosine, sine)
    all_kv = over_chips(jnp.broadcast_to(kv[None], (8, CHIP + 16, 2 * HEAD)).reshape(8 * (CHIP + 16), 2 * HEAD))
    m_one, (all_kv,) = together(gather_one(after(mlp_piece, kv), SLICES), all_kv)

    rows = sds((GROUP * CHIP, HEAD), F32)
    att, wide, lse, k, v, cuts = call(
        fwd_kernel,
        [sds((CHIP, HALF)), rows, rows, sds((SEQ, HEAD)), sds((SEQ, HEAD)), sds((2,), jnp.int32)],
        [SCALARS] + [WHOLE] * 2,
        20,
        out_specs=[WHOLE] * 5 + [SCALARS],
        scratch_shapes=[pltpu.VMEM((GROUP * CHIP, HEAD), F32)] * 3,
    )(meta, q, all_kv.reshape(8, CHIP + 16, 2 * HEAD))

    got, _ = together([(att, "core")])
    att_other = got[0]
    m_two = [send(value, move) for value, move in gather_two([after(p, att) for p in m_one], SLICES)]
    res_mine, res_theirs, atts, wo_turned = call(
        out_kernel,
        [sds((TOK, HALF), F32), sds((TOK, HALF), F32), sds((CHIP, D)), sds((HALF, D))],
        [SCALARS] + [WHOLE] * 10,
        4,
        scratch_shapes=[pltpu.VMEM((D, HALF), BF), pltpu.VMEM((CHIP, HALF), F32)],
    )(meta, att, att_other, piece, *one, *two, *three)
    (res_got,), _ = together([(res_theirs, "core")])
    residual, unit_two = call(
        residual_kernel, [sds((TOK, D), F32), sds((TOK, D))], [SCALARS] + [WHOLE] * 3, 2
    )(meta, tokens, res_mine, res_got)
    _, (unit_two, cots) = together([], unit_two, cots)

    got, m_two = together(gather_one(unit_two, CTX) + [(unit_two, "core")], *m_two)
    one, other = got[:3], got[3:]
    got, _ = together(gather_two(one, CTX) + [(p, "core") for p in one] + gather_three(m_two, SLICES))
    two, other, m_three = got[:3], other + got[3:6], got[6:]
    w, w_turned, w_d, w_part_turned = call(
        weights_kernel,
        [sds((D, 3 * SLOT)), sds((2 * SLOT, D)), sds((SLOT, D)), sds((PART, D))],
        [SCALARS] + [WHOLE] * 9,
        10,
    )(rel_line, mlp_piece, *m_one, *m_two, *m_three, w_part)
    got, (w, w_turned) = together(gather_three(two, CTX) + [(p, "core") for p in two], w, w_turned)
    three, other = got[:1], other + got[1:4]
    twos = [unit_two, *one, *two, *three, *other, send(three[0], "core")]

    u2, hidden, grad_gu, gnt_mine, gnt_other = mlp(rel_ctx, twos, cots, w, w_turned)

    got, _ = together([(gnt_other, "core")])
    q_two = pair_sum(gnt_mine, got[0])
    dw_gu = times_first(after(u2, *got), grad_gu).astype(BF)
    one, (dw_gu,) = together(sum_one(q_two, CTX), dw_gu)
    dw_d = times_first(after(hidden, dw_gu), cots).astype(BF)
    two, (dw_d,) = together(sum_two(q_two, one, CTX), dw_d)
    dealt = call(deal_kernel, [sds((SEND_ROWS, WIDE))] * 8, [SCALARS, WHOLE, WHOLE], 5)(rel_line, dw_gu, dw_d)
    q_mlp = dealt.__getitem__
    three, _ = together(sum_three(q_two, one, two, CTX))

    s_one = [send(value, move) for value, move in sum_one(q_mlp, SLICES)]
    grad_residual, gao_mine, gao_theirs = call(
        norm_two_kernel,
        [sds((TOK, D), F32), sds((TOK, HALF)), sds((TOK, HALF))],
        [SCALARS] + [WHOLE] * 6,
        2,
        scratch_shapes=[pltpu.VMEM((TOK, D), BF)],
    )(meta, q_two(0), two[2], three[0], three[1], residual, cot)
    (gao_got,), _ = together([(gao_theirs, "core")])
    ga_mine, ga_theirs, gaos = call(
        out_grad_kernel,
        [sds((CHIP, HALF), F32), sds((CHIP, HALF)), sds((CHIP, HALF))],
        [SCALARS] + [WHOLE] * 3,
        3,
        scratch_shapes=[pltpu.VMEM((CHIP, D), F32)],
    )(meta, gao_mine, gao_got, wo_turned)
    (ga_got,), _ = together([(ga_theirs, "core")])

    stacked = pltpu.VMEM((GROUP * CHIP, HEAD), F32)
    dq, dkv = call(
        bwd_kernel,
        [sds((CHIP, HALF)), sds((SEQ, 2 * HEAD))],
        [SCALARS] * 2 + [WHOLE] * 9,
        28,
        scratch_shapes=[
            pltpu.VMEM((GROUP * CHIP, HEAD), BF),
            stacked,
            pltpu.VMEM((GROUP * CHIP, BK), BF),
            pltpu.VMEM((GROUP * CHIP, BK), BF),
            stacked,
            pltpu.VMEM((SEQ, HEAD), F32),
            pltpu.VMEM((SEQ, HEAD), F32),
        ],
    )(meta, cuts, q, k, v, wide, lse, cosine, sine, ga_mine, ga_got)
    _, (dq, dkv, *s_one) = together([], dq, dkv, *s_one)

    all_dkv = over_chips(dkv)
    down_mine, down_other = through_down(rel_ctx, after(hidden, dkv), w_d)
    s_two, (all_dkv, down_mine, down_other) = together(
        sum_two(q_mlp, s_one, SLICES), all_dkv, down_mine, down_other
    )
    s_three = [send(value, move) for value, move in sum_three(q_mlp, s_one, s_two, SLICES)]

    gu1_mine, gu1_theirs, *pieces = call(
        project_grad_kernel,
        [sds((TOK, D), F32), sds((TOK, D))] + [sds((ROWS + 16, PART + HALF))] * 8,
        [SCALARS] + [WHOLE] * 8,
        9,
        scratch_shapes=[pltpu.VMEM((CHIP, PART), BF), pltpu.VMEM((D, PART + HALF), BF), pltpu.VMEM((CHIP, D), F32)],
    )(meta, all_dkv, dq, units, w_part_turned, cosine, sine, atts, gaos)
    q_attn = pieces.__getitem__

    got, s_three = together(sum_one(q_attn, SLICES) + [(gu1_theirs, "core"), (down_other, "core")], *s_three)
    a_one, q_down = got[:2], pair_sum(down_mine, got[3])
    mine = call(slice_sum_kernel, sds((SEND_ROWS, WIDE)), [WHOLE] * 6, 3)(
        q_mlp(0), s_two[2], *s_three, gu_own, gain_two
    )
    mlp_grads = lax.all_gather(mine, "context", axis=0)
    grad_tokens = call(norm_one_kernel, sds((TOK, D)), [WHOLE] * 4, 2)(gu1_mine, got[2], tokens, grad_residual)
    a_two, (grad_tokens, mine) = together(sum_two(q_attn, a_one, SLICES), grad_tokens, mine)
    d_one = [send(after(value, mine), move) for value, move in sum_one(q_down, CTX)]
    a_three, d_one = together(sum_three(q_attn, a_one, a_two, SLICES), *d_one)

    dealt = call(
        line_deal_kernel,
        sds((8, ROWS + 16, 2 * HEAD)),
        [WHOLE] * 4,
        3,
        scratch_shapes=[pltpu.VMEM((ROWS + 16, PART + HALF), F32)],
    )(q_attn(0), a_two[2], *a_three)
    blocks = over_chips(dealt)
    d_two = [send(after(value, dealt), move) for value, move in sum_two(q_down, d_one, CTX)]
    mine = call(block_kernel, sds((ROWS + 16, 2 * HEAD)), [SCALARS] + [WHOLE] * 5, 2)(
        meta, blocks, w_query, w_key, w_value, gain_one
    )

    attn_mine = over_chips(jnp.broadcast_to(mine[None], (8, ROWS + 16, 2 * HEAD)))
    _, (mine, *d_two) = together([], mine, *d_two)
    d_three = [send(value, move) for value, move in sum_three(q_down, d_one, d_two, CTX)]
    (attn_other,), (attn_mine,) = together([(attn_mine, "core")], attn_mine)
    output = (residual + sum_all(q_down, d_two, d_three)).astype(BF)


    wanted = jnp.arange(NCTX, dtype=jnp.int32)

    slots = wanted ^ (2 * yh)
    grad_gate_w, grad_up_w, gain_two_cols = gate_up_out(slots, mlp_grads)
    grad_down_w = down_out(slots, mlp_grads)
    attn_mine, attn_other = after(attn_mine, grad_gate_w), after(attn_other, grad_gate_w)
    grad_wq, grad_wk, grad_wv, grad_wo, sum_bq, sum_bk, sum_bv, grad_gain_one = call(
        attn_kernel,
        [
            sds((ROWS, D), F32),
            sds((ROWS, 256), F32),
            sds((ROWS, 256), F32),
            sds((ROWS, D), F32),
            sds((1, ROWS), F32),
            sds((1, 32), F32),
            sds((1, 32), F32),
            sds((1, ROWS), F32),
        ],
        [SCALARS, WHOLE, WHOLE],
        4,
        scratch_shapes=[
            pltpu.VMEM((8, D), F32),
            pltpu.VMEM((2, 8, 256), F32),
        ],
    )(jnp.stack([f, core]).astype(jnp.int32), attn_mine, attn_other)
    return (
        output[None],
        grad_tokens[None],
        grad_gain_one[0],
        grad_wq,
        sum_bq[0],
        grad_wk,
        sum_bk[0],
        grad_wv,
        sum_bv[0],
        grad_wo,
        gain_two_cols[:, HEAD - 1],
        grad_gate_w,
        grad_up_w,
        grad_down_w,
    )


def solution(mesh):
    tokens = P("fsdp", "context", None)
    matrix, vector = P("fsdp", None), P("fsdp")
    weights = (vector, matrix, vector, matrix, vector, matrix, vector, matrix, vector, matrix, matrix, matrix)
    return jax.shard_map(
        on_device,
        mesh=mesh,
        in_specs=(tokens, P("fsdp", "context"), *weights, tokens),
        out_specs=(tokens, tokens, *weights),
        check_vma=False,
    )
```

```python
import math

import jax
import jax.numpy as jnp
import numpy as np
from jax import lax
from jax.experimental import pallas as pl
from jax.experimental.pallas import tpu as pltpu
from jax.sharding import PartitionSpec as P

D = 1536
FF = 8960
HEADS = 12
KV_HEADS = 2
HEAD = 128
GROUP = HEADS // KV_HEADS
HALF = D // 2
PART = HALF + 2 * HEAD
SEQ = 2048
EPS = 1e-06
THETA = 1000000.0
NCTX, NFS = 16, 8
TOK = SEQ // NCTX
ROWS = D // NFS
BLOCK = FF // NFS // NCTX
PIECE = 80
SLOT = NFS * PIECE
SEND_ROWS = ROWS + PIECE + 16
AXES = ("context", "fsdp")
SCALE = 1.0 / math.sqrt(HEAD)
LOG2E = math.log2(math.e)
CHIP = 256
BK = 512
BF, F32 = jnp.bfloat16, jnp.float32
VMEM_BYTES = 58 * 1024 * 1024
NEG = -1e30


def split_place(c, f):
    return c // 4, (c // 2) % 2, c % 2, f // 2, f % 2


def pairs_of(move):
    pairs = []
    for c in range(NCTX):
        for f in range(NFS):
            x, yl, core, z, yh = move(*split_place(c, f))
            pairs.append((c * NFS + f, ((x % 4) * 4 + (yl % 2) * 2 + core % 2) * NFS + (z % 4) * 2 + yh % 2))
    return pairs


MOVES = {
    "x+": pairs_of(lambda x, yl, core, z, yh: (x + 1, yl, core, z, yh)),
    "x-": pairs_of(lambda x, yl, core, z, yh: (x - 1, yl, core, z, yh)),
    "yl": pairs_of(lambda x, yl, core, z, yh: (x, yl + 1, core, z, yh)),
    "core": pairs_of(lambda x, yl, core, z, yh: (x, yl, core + 1, z, yh)),
    "z+": pairs_of(lambda x, yl, core, z, yh: (x, yl, core, z + 1, yh)),
    "z-": pairs_of(lambda x, yl, core, z, yh: (x, yl, core, z - 1, yh)),
    "yw": pairs_of(lambda x, yl, core, z, yh: (x, yl + 1, core, z, yh + 1)),
}
SAME_CORE = [[c for c in range(NCTX) if c % 2 == core] for core in range(2)]


def send(value, move):
    pairs = MOVES[move] if isinstance(move, str) else move
    return lax.ppermute(value, AXES, pairs)


def add(*terms):
    total = terms[0].astype(F32)
    for t in terms[1:]:
        total = total + t.astype(F32)
    return total


def after(value, *earlier):
    return lax.optimization_barrier((value, *earlier))[0]


def together(sends, *rest):
    got = [send(value, move) for value, move in sends]
    done = lax.optimization_barrier((*got, *rest))
    return list(done[: len(got)]), list(done[len(got) :])


REL8 = [(0, 0), (-1, 0), (1, 0), (0, 1), (-1, 1), (2, 0), (1, 1), (2, 1)]
CTX, SLICES = ("x+", "x-", "yl"), ("z+", "z-", "yw")


def over_chips(terms):
    return lax.all_to_all(terms, "context", 0, 0, axis_index_groups=SAME_CORE, tiled=True)


def gather_one(v, way):
    return [(v, way[0]), (v, way[1]), (v, way[2])]


def gather_two(parts, way):
    _, b, c = parts
    return [(c, way[0]), (b, way[1]), (b, way[2])]


def gather_three(parts, way):
    return [(parts[1], way[2])]


def sum_one(q, way):
    return [(q(7), way[2]), (q(4), way[1])]


def sum_two(q, got, way):
    later = [after(q(j), *got[:2]) for j in (6, 1)]
    return [(add(q(5), got[0]).astype(BF), way[0]), (later[0], way[2]), (later[1], way[1])]


def sum_three(q, one, two, way):
    return [(add(q(2), two[0], two[1]).astype(BF), way[0]), (add(q(3), one[1]).astype(BF), way[2])]


def sum_all(q, two, three):
    return add(q(0), two[2], three[0], three[1])


def pair_sum(mine, other):
    n = mine.shape[0] // 8
    return lambda j: add(mine[j * n : (j + 1) * n], other[j * n : (j + 1) * n]).astype(BF)


def times_last(left, right):
    return lax.dot_general(left, right, (((1,), (1,)), ((), ())), preferred_element_type=F32)


def times_first(left, right):
    return lax.dot_general(left, right, (((0,), (0,)), ((), ())), preferred_element_type=F32)


def dot(left, right):
    return jnp.dot(left, right, preferred_element_type=F32)


def sds(shape, dtype=BF):
    return jax.ShapeDtypeStruct(shape, dtype)


WHOLE = pl.BlockSpec(memory_space=pltpu.VMEM)
SCALARS = pl.BlockSpec(memory_space=pltpu.SMEM)
ANYWHERE = pl.BlockSpec(memory_space=pl.ANY)


def call(kernel, out_shape, specs, us, **kw):
    return pl.pallas_call(
        kernel,
        out_shape=out_shape,
        in_specs=specs,
        compiler_params=pltpu.CompilerParams(vmem_limit_bytes=VMEM_BYTES),
        cost_estimate=pl.CostEstimate(flops=int(us * 1.0e9), bytes_accessed=int(us * 1e5), transcendentals=0),
        **kw,
    )


def first_kernel(
    at, tokens, ids, w_query, w_key, w_value, w_out, gain, b_query, b_key, b_value, unit, piece, wide, narrow
):
    f, core = at[0], at[1]
    x = tokens[...].astype(F32)
    unit[:TOK, :] = (x * lax.rsqrt(jnp.mean(x * x, axis=1, keepdims=True) + EPS)).astype(BF)
    lane = lax.broadcasted_iota(jnp.int32, (16, D), 1)
    before = [jnp.sum((ids[...] < n).astype(F32), axis=1, keepdims=True) for n in (1, 2)]
    unit[TOK:, :] = jnp.where(lane == 0, before[0], jnp.where(lane == 1, before[1], 0.0)).astype(BF)
    scale = gain[...]
    qs = pl.ds(pl.multiple_of(core * HALF, HALF), HALF)
    ks = pl.ds(pl.multiple_of(core * HEAD, HEAD), HEAD)
    piece[:ROWS, :HALF] = (w_query[:, qs].astype(F32) * scale).astype(BF)
    piece[:ROWS, HALF : HALF + HEAD] = (w_key[:, ks].astype(F32) * scale).astype(BF)
    piece[:ROWS, PART:] = w_out[:, qs]
    piece[:ROWS, HALF + HEAD : PART] = (w_value[:, ks].astype(F32) * scale).astype(BF)
    piece[ROWS:, :] = jnp.zeros((16, PART + HALF), BF)
    wide[...] = jnp.zeros_like(wide)
    wide[0:1, :ROWS] = b_query[...]
    wide[...] = pltpu.roll(wide[...], f * ROWS, 1)
    piece[ROWS : ROWS + 8, :HALF] = wide[:, qs].astype(BF)
    for b, at_col in ((b_key, HALF), (b_value, HALF + HEAD)):
        narrow[...] = jnp.zeros_like(narrow)
        narrow[0:1, :32] = b[...]
        narrow[...] = pltpu.roll(narrow[...], f * 32, 1)
        piece[ROWS : ROWS + 8, at_col : at_col + HEAD] = narrow[:, ks].astype(BF)


def both_cores(core, mine, theirs, out):
    n = mine.shape[0]
    out[pl.ds(pl.multiple_of(core * n, n), n), :] = mine
    out[pl.ds(pl.multiple_of((1 - core) * n, n), n), :] = theirs


def rotated(y, cosine, sine):
    return y * cosine + pltpu.roll(y, HEAD // 2, 1) * sine


def project_kernel(meta, unit, unit_other, *refs):
    parts, (cosine, sine, q, kv, w, units) = refs[:8], refs[8:]
    core, chip = meta[0], meta[1]
    both_cores(core, unit[:TOK, :], unit_other[:TOK, :], units)
    bias = jnp.zeros((1, PART), F32)
    for j in range(8):
        w[pl.ds(pl.multiple_of(meta[2 + j] * ROWS, ROWS), ROWS), :] = parts[j][:ROWS, :PART]
        bias += parts[j][ROWS:, :PART].astype(F32)[:1]
    y = dot(units[...], w[...]) + bias
    here = pl.ds(pl.multiple_of(chip * CHIP, CHIP), CHIP)
    cos_rows, sin_rows = cosine[here, :], sine[here, :]
    for h in range(GROUP):
        turned = rotated(y[:, h * HEAD : (h + 1) * HEAD], cos_rows, sin_rows)
        q[h * CHIP : (h + 1) * CHIP, :] = (turned * (SCALE * LOG2E)).astype(BF)
    keys = rotated(y[:, HALF : HALF + HEAD], cos_rows, sin_rows).astype(BF)
    vals = y[:, HALF + HEAD :].astype(BF)
    counts = unit[TOK:, : 2 * HEAD].astype(F32) + unit_other[TOK:, : 2 * HEAD].astype(F32)
    for to in range(8):
        kv[to, :CHIP, :HEAD] = keys
        kv[to, :CHIP, HEAD:] = vals
        kv[to, CHIP:, :] = counts.astype(BF)


def doc_begins(cuts, places):
    return jnp.where(places < cuts[0], 0, jnp.where(places < cuts[1], cuts[0], cuts[1]))


def visible_keys(cuts, chip, kb):
    places = chip * CHIP + lax.broadcasted_iota(jnp.int32, (CHIP, 1), 0)
    keys = kb * BK + lax.broadcasted_iota(jnp.int32, (1, BK), 1)
    return (keys <= places) & (keys >= doc_begins(cuts, places))


def key_blocks(cuts, chip):
    return doc_begins(cuts, chip * CHIP) // BK, chip // (BK // CHIP) + 1


def fwd_kernel(meta, q, *refs):
    parts, out, wide, lse, k, v, cuts_out, top, total, acc = refs
    chip = meta[1]
    lane = lax.broadcasted_iota(jnp.int32, (1, HEAD), 1)
    counts = sum(parts[j, CHIP:, :HEAD].astype(F32) for j in range(8))[:1]
    cuts = [jnp.sum(jnp.where(lane == i, counts, 0.0)).astype(jnp.int32) for i in range(2)]
    cuts_out[0], cuts_out[1] = cuts
    for j in range(8):
        there = slice(j * CHIP, (j + 1) * CHIP)
        k[there, :] = parts[j, :CHIP, :HEAD]
        v[there, :] = parts[j, :CHIP, HEAD:]
    top[...] = jnp.full_like(top, NEG)
    total[...] = jnp.zeros_like(total)
    acc[...] = jnp.zeros_like(acc)

    def step(kb, _):
        there = pl.ds(pl.multiple_of(kb * BK, BK), BK)
        keys, vals = k[there, :], v[there, :]
        visible = visible_keys(cuts, chip, kb)
        for h in range(GROUP):
            rows = slice(h * CHIP, (h + 1) * CHIP)
            s = jnp.where(visible, times_last(q[rows, :], keys), NEG)
            old = top[rows, :]
            new = jnp.maximum(old, jnp.max(s, axis=1, keepdims=True))
            p = jnp.exp2(s - new[:, :1])
            fade = jnp.exp2(old - new)
            top[rows, :] = new
            total[rows, :] = total[rows, :] * fade + jnp.sum(p, axis=1, keepdims=True)
            acc[rows, :] = acc[rows, :] * fade + dot(p.astype(BF), vals)
        return 0

    lo, hi = key_blocks(cuts, chip)
    lax.fori_loop(lo, hi, step, 0)
    for h in range(GROUP):
        rows, cols = slice(h * CHIP, (h + 1) * CHIP), slice(h * HEAD, (h + 1) * HEAD)
        result = acc[rows, :] / total[rows, :]
        out[:, cols] = result.astype(BF)
        wide[rows, :] = result
        lse[rows, :] = top[rows, :] + jnp.log2(total[rows, :])


def bwd_kernel(meta, cuts_in, q, k, v, wide, lse, cosine, sine, grad, grad_other, dq_out, dkv, go, delta, p_all, ds_all, dq, dk, dv):
    core, chip = meta[0], meta[1]
    cuts = (cuts_in[0], cuts_in[1])
    dq[...] = jnp.zeros_like(dq)
    dk[...] = jnp.zeros_like(dk)
    dv[...] = jnp.zeros_like(dv)
    for h in range(GROUP):
        rows, cols = slice(h * CHIP, (h + 1) * CHIP), slice(h * HEAD, (h + 1) * HEAD)
        low = (grad[:, cols] + grad_other[:, cols].astype(F32)).astype(BF)
        go[rows, :] = low
        found = jnp.sum(low.astype(F32) * wide[rows, :], axis=1, keepdims=True)
        delta[rows, :] = jnp.broadcast_to(found, (CHIP, HEAD))

    def step(kb, _):
        there = pl.ds(pl.multiple_of(kb * BK, BK), BK)
        keys, vals = k[there, :], v[there, :]
        visible = visible_keys(cuts, chip, kb)
        for h in range(GROUP):
            rows = slice(h * CHIP, (h + 1) * CHIP)
            s = jnp.where(visible, times_last(q[rows, :], keys), NEG)
            p = jnp.exp2(s - lse[rows, :1])
            dp = times_last(go[rows, :], vals)
            ds = (p * (dp - delta[rows, :1])).astype(BF)
            p_all[rows, :] = p.astype(BF)
            ds_all[rows, :] = ds
            dq[rows, :] += dot(ds, keys)
        dv[there, :] = times_first(p_all[...], go[...])
        dk[there, :] = times_first(ds_all[...], q[...])
        return 0

    lo, hi = key_blocks(cuts, chip)
    lax.fori_loop(lo, hi, step, 0)
    here = pl.ds(pl.multiple_of(chip * CHIP, CHIP), CHIP)
    cos_rows, sin_rows = cosine[here, :], -sine[here, :]
    for h in range(GROUP):
        rows, cols = slice(h * CHIP, (h + 1) * CHIP), slice(h * HEAD, (h + 1) * HEAD)
        dq_out[:, cols] = rotated(dq[rows, :] * SCALE, cos_rows, sin_rows).astype(BF)
    dkv[:, :HEAD] = (dk[...] * (1.0 / LOG2E)).astype(BF)
    dkv[:, HEAD:] = dv[...].astype(BF)


def out_kernel(meta, att, att_other, *refs):
    parts, (mine, theirs, atts, w_turned, w, held) = refs[:8], refs[8:]
    core = meta[0]
    atts[:, pl.ds(pl.multiple_of(core * HALF, HALF), HALF)] = att[...]
    atts[:, pl.ds(pl.multiple_of((1 - core) * HALF, HALF), HALF)] = att_other[...]
    for j in range(8):
        w[pl.ds(pl.multiple_of(meta[2 + j] * ROWS, ROWS), ROWS), :] = parts[j][:ROWS, PART:]
    held[...] = dot(atts[...], w[...])
    mine[...] = held[pl.ds(pl.multiple_of(core * TOK, TOK), TOK), :]
    theirs[...] = held[pl.ds(pl.multiple_of((1 - core) * TOK, TOK), TOK), :]
    for i in range(HALF // 256):
        cols = slice(i * 256, (i + 1) * 256)
        w_turned[cols, :] = jnp.transpose(w[:, cols])


def residual_kernel(meta, tokens, mine, got, residual, unit):
    core = meta[0]
    here = pl.ds(pl.multiple_of(core * HALF, HALF), HALF)
    there = pl.ds(pl.multiple_of((1 - core) * HALF, HALF), HALF)
    residual[:, here] = tokens[:, here].astype(F32) + mine[...]
    residual[:, there] = tokens[:, there].astype(F32) + got[...]
    x = residual[...]
    unit[...] = (x * lax.rsqrt(jnp.mean(x * x, axis=1, keepdims=True) + EPS)).astype(BF)


def norm_grad(x, grad):
    scale = lax.rsqrt(jnp.mean(x * x, axis=1, keepdims=True) + EPS)
    unit = x * scale
    return scale * (grad - unit * jnp.mean(grad * unit, axis=1, keepdims=True))


def norm_two_kernel(meta, term, a, b, c, residual, cot, grad_residual, mine, theirs, held):
    core = meta[0]
    grad = add(term[...], a[...], b[...], c[...])
    result = cot[...].astype(F32) + norm_grad(residual[...], grad)
    grad_residual[...] = result
    held[...] = result.astype(BF)
    mine[...] = held[:, pl.ds(pl.multiple_of(core * HALF, HALF), HALF)]
    theirs[...] = held[:, pl.ds(pl.multiple_of((1 - core) * HALF, HALF), HALF)]


def out_grad_kernel(meta, grad, grad_other, w_turned, mine, theirs, grads, held):
    core = meta[0]
    both_cores(core, grad[...], grad_other[...], grads)
    held[...] = dot(grads[...], w_turned[...])
    mine[...] = held[:, pl.ds(pl.multiple_of(core * HALF, HALF), HALF)]
    theirs[...] = held[:, pl.ds(pl.multiple_of((1 - core) * HALF, HALF), HALF)].astype(BF)


def project_grad_kernel(meta, terms, dq, units, w_turned, cosine, sine, atts, grads, mine, theirs, *refs):
    pieces, (both, dw, held) = refs[:8], refs[8:]
    core, chip = meta[0], meta[1]
    here = pl.ds(pl.multiple_of(chip * CHIP, CHIP), CHIP)
    dkv = add(*[terms[j * CHIP : (j + 1) * CHIP, :] for j in range(8)])
    both[:, :HALF] = dq[...]
    both[:, HALF : HALF + HEAD] = rotated(dkv[:, :HEAD], cosine[here, :], -sine[here, :]).astype(BF)
    both[:, HALF + HEAD :] = dkv[:, HEAD:].astype(BF)
    held[...] = dot(both[...], w_turned[...])
    mine[...] = held[pl.ds(pl.multiple_of(core * TOK, TOK), TOK), :]
    theirs[...] = held[pl.ds(pl.multiple_of((1 - core) * TOK, TOK), TOK), :].astype(BF)
    dw[:, :PART] = times_first(units[...], both[...]).astype(BF)
    dw[:, PART:] = times_first(atts[...], grads[...]).astype(BF)
    bias = jnp.sum(both[...].astype(F32), axis=0, keepdims=True)
    bias = jnp.broadcast_to(bias, (16, PART)).astype(BF)
    for j, out in enumerate(pieces):
        out[:ROWS, :] = dw[pl.ds(pl.multiple_of(meta[2 + j] * ROWS, ROWS), ROWS), :]
        out[ROWS:, :PART] = bias
        out[ROWS:, PART:] = jnp.zeros((16, HALF), BF)


def norm_one_kernel(mine, got, tokens, grad_residual, out):
    grad = mine[...] + got[...].astype(F32)
    out[...] = (grad_residual[...] + norm_grad(tokens[...].astype(F32), grad)).astype(BF)


def line_deal_kernel(term, a, b, c, *refs):
    out, total = refs
    total[...] = add(term[...], a[...], b[...], c[...])
    for chip in range(8):
        out[chip, :, :HEAD] = total[:, chip * HEAD : (chip + 1) * HEAD].astype(BF)
        at = PART + min(chip, GROUP - 1) * HEAD
        out[chip, :, HEAD:] = total[:, at : at + HEAD].astype(BF)


def block_kernel(meta, terms, w_query, w_key, w_value, gain, out):
    core, chip = meta[0], meta[1]
    total = add(*[terms[j] for j in range(8)])
    head = core * GROUP + jnp.minimum(chip, GROUP - 1)
    wq = w_query[:, pl.ds(pl.multiple_of(head * HEAD, HEAD), HEAD)].astype(F32)
    ks = pl.ds(pl.multiple_of(core * HEAD, HEAD), HEAD)
    wk, wv = w_key[:, ks].astype(F32), w_value[:, ks].astype(F32)
    w = jnp.where(chip < GROUP, wq, jnp.where(chip == GROUP, wk, wv))
    grad = total[:ROWS, :HEAD]
    for_gain = jnp.sum(grad * w, axis=1, keepdims=True)
    for_gain = jnp.transpose(jnp.broadcast_to(for_gain, (ROWS, HEAD)))
    low = (grad * gain[...]).astype(BF)
    beside = total[:ROWS, HEAD:].astype(BF)
    row = lax.broadcasted_iota(jnp.int32, (16, 2 * HEAD), 0)
    gains = jnp.concatenate([for_gain[:16, :], jnp.zeros((16, 2 * HEAD - ROWS), F32)], axis=1)
    below = jnp.where(row == 0, total[ROWS:, :], gains).astype(BF)
    for to in range(8):
        out[to, :ROWS, :HEAD] = low
        out[to, :ROWS, HEAD:] = beside
        out[to, ROWS:, :] = below


def attn_kernel(slots, *refs):
    held, wq, wk, wv, wo, bq, bk, bv, gain, wide, narrow = refs[0:2], *refs[2:]
    f, mine = slots[0], slots[1]
    total = jnp.zeros((16, 2 * HEAD), F32)
    for core in range(2):
        cols = slice(core * HEAD, (core + 1) * HEAD)
        for chip in range(8):
            block = jnp.where(mine == core, held[0][chip], held[1][chip]).astype(F32)
            total += block[ROWS:, :]
            if chip < GROUP:
                at = slice((core * GROUP + chip) * HEAD, (core * GROUP + chip + 1) * HEAD)
                wq[:, at] = block[:ROWS, :HEAD]
                wo[:, at] = block[:ROWS, HEAD:]
                wide[:, at] = block[ROWS : ROWS + 8, :HEAD]
            else:
                out, i = ((wk, 0), (wv, 1))[chip - GROUP]
                out[:, cols] = block[:ROWS, :HEAD]
                narrow[i, :, cols] = block[ROWS : ROWS + 8, :HEAD]
    gain[...] = total[1:2, :ROWS]
    bq[...] = pltpu.roll(wide[...], D - f * ROWS, 1)[:1, :ROWS]
    bk[...] = pltpu.roll(narrow[0], 256 - f * 32, 1)[:1, :32]
    bv[...] = pltpu.roll(narrow[1], 256 - f * 32, 1)[:1, :32]


WIDE = 2 * SLOT
TAIL = D - WIDE


def slice_kernel(at, w_gate, w_up, w_down, gain, out, own, gathered):
    lane = lax.broadcasted_iota(jnp.int32, (ROWS, PIECE), 1)
    for i, w in enumerate((w_gate, w_up)):
        for j in range(NFS):
            start = j * (FF // NFS) + at[0] * BLOCK
            base = jnp.minimum(start // 128 * 128, FF - 256)
            window = w[:, pl.ds(pl.multiple_of(base, 128), 256)].astype(F32)
            window = pltpu.roll(window, 256 - (start - base), 1)[:, :PIECE]
            gathered[:, i * SLOT + j * PIECE : i * SLOT + (j + 1) * PIECE] = jnp.where(lane < BLOCK, window, 0.0)
    own[...] = gathered[...].astype(BF)
    out[:ROWS, :] = (gathered[...] * gain[...]).astype(BF)
    start = at[0] * BLOCK
    base = jnp.minimum(start // 16 * 16, FF // NFS - 96)
    window = w_down[pl.ds(pl.multiple_of(base, 16), 96), :].astype(F32)
    window = pltpu.roll(window, 96 - (start - base), 0)[:PIECE]
    row = lax.broadcasted_iota(jnp.int32, (PIECE, D), 0)
    put_down(out, jnp.where(row < BLOCK, window, 0.0).astype(BF))


def put_down(out, rows):
    out[ROWS : ROWS + PIECE, :] = rows[:, :WIDE]
    for i in range(PIECE // 16):
        out[ROWS + PIECE :, i * TAIL : (i + 1) * TAIL] = rows[i * 16 : (i + 1) * 16, WIDE:]


def take_down(part, at):
    tail = [part[at + PIECE :, i * TAIL : (i + 1) * TAIL] for i in range(PIECE // 16)]
    return jnp.concatenate([part[at : at + PIECE, :], jnp.concatenate(tail, axis=0)], axis=1)


def weights_kernel(order, *refs):
    parts, qkv = refs[:8], refs[8]
    w, w_turned, down, qkv_turned = refs[9:]
    for j in range(8):
        w[pl.ds(pl.multiple_of(order[j] * ROWS, ROWS), ROWS), :WIDE] = parts[j][:ROWS, :]
        down[pl.ds(pl.multiple_of(order[j] * PIECE, 16), PIECE), :] = take_down(parts[j], ROWS)
    for i in range(WIDE // 256):
        w_turned[i * 256 : (i + 1) * 256, :] = jnp.transpose(w[:, i * 256 : (i + 1) * 256])
    for i in range(SLOT // 128):
        w[:, WIDE + i * 128 : WIDE + (i + 1) * 128] = jnp.transpose(down[i * 128 : (i + 1) * 128, :])
    for i in range(PART // 256):
        qkv_turned[i * 256 : (i + 1) * 256, :] = jnp.transpose(qkv[:, i * 256 : (i + 1) * 256])


def deal_kernel(order, gate, up, down, *outs):
    for j, out in enumerate(outs):
        here = pl.ds(pl.multiple_of(order[j] * ROWS, ROWS), ROWS)
        out[:ROWS, :SLOT] = gate[here, :]
        out[:ROWS, SLOT:] = up[here, :]
        put_down(out, down[pl.ds(pl.multiple_of(order[j] * PIECE, 16), PIECE), :])


def slice_sum_kernel(term, a, b, c, own, gain, out):
    total = add(term[...], a[...], b[...], c[...])
    grad = total[:ROWS, :]
    for_gain = jnp.sum(grad * own[...].astype(F32), axis=1, keepdims=True)
    lane = lax.broadcasted_iota(jnp.int32, (ROWS, WIDE), 1)
    out[:ROWS, :] = jnp.where(lane == SLOT - 1, for_gain, grad * gain[...]).astype(BF)
    out[ROWS:, :] = total[ROWS:, :].astype(BF)


MB = 256


def mlp_kernel(meta, *refs):
    us, (cots, w_in, w_turned_in) = refs[:16], refs[16:19]
    u_out, hidden_out, gate_out, up_out, mine_out, other_out = refs[19:25]
    u, c, hidden, grad, res, w, w_turned, in_sem, out_sem = refs[25:]

    def rows_of(i, n):
        return pl.ds(pl.multiple_of(i * n, n), n)

    loads = [
        pltpu.make_async_copy(w_in, w, in_sem.at[32]),
        pltpu.make_async_copy(w_turned_in, w_turned, in_sem.at[33]),
    ]
    for load in loads:
        load.start()
    for r in range(16):
        here = pl.ds(r * TOK, TOK)
        pltpu.make_async_copy(us[r], u.at[here, :], in_sem.at[r]).start()
        pltpu.make_async_copy(cots.at[rows_of(meta[r], TOK), :], c.at[here, :], in_sem.at[16 + r]).start()
    for load in loads:
        load.wait()

    def results(i):
        rows = rows_of(i, MB)
        return [
            pltpu.make_async_copy(u.at[rows, :], u_out.at[rows, :], out_sem.at[7 * i]),
            pltpu.make_async_copy(grad.at[rows, pl.ds(0, SLOT)], gate_out.at[rows, :], out_sem.at[7 * i + 1]),
            pltpu.make_async_copy(grad.at[rows, pl.ds(SLOT, SLOT)], up_out.at[rows, :], out_sem.at[7 * i + 5]),
        ] + [
            pltpu.make_async_copy(
                hidden.at[rows_of(2 * i + h, TOK), :],
                hidden_out.at[rows_of(meta[2 * i + h], TOK), :],
                out_sem.at[7 * i + 2 + h],
            )
            for h in range(2)
        ]

    def last(i, to):
        return pltpu.make_async_copy(res.at[rows_of(i, MB), :], to.at[rows_of(lax.rem(i, 4), MB), :], out_sem.at[7 * i + 4])

    def step(i, _):
        for h in range(2):
            rows = rows_of(2 * i + h, TOK)
            pltpu.make_async_copy(us[0], u.at[rows, :], in_sem.at[2 * i + h]).wait()
            pltpu.make_async_copy(us[0], c.at[rows, :], in_sem.at[16 + 2 * i + h]).wait()
        rows = rows_of(i, MB)
        x = u[rows, :]
        gate = dot(x, w[:, :SLOT])
        upward = dot(x, w[:, SLOT : 2 * SLOT])
        back = dot(c[rows, :], w[:, 2 * SLOT :])
        sig = jax.nn.sigmoid(gate)
        swished = gate * sig
        hidden[rows, :] = (swished * upward).astype(BF)
        grad[rows, :SLOT] = (back * upward * sig * (1.0 + gate * (1.0 - sig))).astype(BF)
        grad[rows, SLOT:] = (back * swished).astype(BF)
        for one in results(i):
            one.start()
        res[rows, :] = dot(grad[rows, :], w_turned[...]).astype(BF)

        @pl.when(i < 4)
        def _():
            last(i, mine_out).start()

        @pl.when(i >= 4)
        def _():
            last(i, other_out).start()

        return 0

    lax.fori_loop(0, SEQ // MB, step, 0)

    def finish(i, _):
        for one in results(i):
            one.wait()
        last(i, mine_out).wait()
        return 0

    lax.fori_loop(0, SEQ // MB, finish, 0)


def mlp(meta, us, cots, w, w_turned):
    return call(
        mlp_kernel,
        [sds((SEQ, D))] + [sds((SEQ, SLOT))] * 3 + [sds((SEQ // 2, D))] * 2,
        [SCALARS] + [ANYWHERE] * 19,
        25,
        out_specs=[ANYWHERE] * 6,
        scratch_shapes=[
            pltpu.VMEM((SEQ, D), BF),
            pltpu.VMEM((SEQ, D), BF),
            pltpu.VMEM((SEQ, SLOT), BF),
            pltpu.VMEM((SEQ, 2 * SLOT), BF),
            pltpu.VMEM((SEQ, D), BF),
            pltpu.VMEM((D, 3 * SLOT), BF),
            pltpu.VMEM((2 * SLOT, D), BF),
            pltpu.SemaphoreType.DMA((34,)),
            pltpu.SemaphoreType.DMA((56,)),
        ],
    )(meta, *us, cots, w, w_turned)


def through_down_kernel(order, hidden, w, mine, other):
    def step(i, _):
        rows = [hidden[pl.ds(pl.multiple_of(order[2 * i + h] * TOK, TOK), TOK), :] for h in range(2)]
        result = dot(jnp.concatenate(rows, axis=0), w[...]).astype(BF)
        there = pl.ds(pl.multiple_of(lax.rem(i, 4) * MB, MB), MB)

        @pl.when(i < 4)
        def _():
            mine[there, :] = result

        @pl.when(i >= 4)
        def _():
            other[there, :] = result

        return 0

    lax.fori_loop(0, SEQ // MB, step, 0)


def through_down(order, hidden, w):
    return call(through_down_kernel, [sds((SEQ // 2, D)), sds((SEQ // 2, D))], [SCALARS, WHOLE, WHOLE], 8)(
        order, hidden, w
    )


def gate_up_kernel(slots, *refs):
    held, gate, up, gain = refs
    total = jnp.zeros((gain.shape[0], HEAD), F32)
    for s in range(16):
        block = held[slots[s]]
        for i, out in enumerate((gate, up)):
            wide = block[:, i * SLOT : (i + 1) * SLOT].astype(F32)
            for j in range(NFS):
                at = j * (FF // NFS) + s * BLOCK
                out[:, at : at + BLOCK] = wide[:, j * PIECE : j * PIECE + BLOCK]
        total += block[:, SLOT - HEAD : SLOT].astype(F32)
    gain[...] = total


def gate_up_out(slots, parts):
    step = 32
    return pl.pallas_call(
        gate_up_kernel,
        grid_spec=pltpu.PrefetchScalarGridSpec(
            num_scalar_prefetch=1,
            grid=(ROWS // step,),
            in_specs=[pl.BlockSpec((NCTX, step, WIDE), lambda i, s: (0, i, 0))],
            out_specs=[
                pl.BlockSpec((step, FF), lambda i, s: (i, 0)),
                pl.BlockSpec((step, FF), lambda i, s: (i, 0)),
                pl.BlockSpec((step, HEAD), lambda i, s: (i, 0)),
            ],
        ),
        out_shape=[sds((ROWS, FF), F32), sds((ROWS, FF), F32), sds((ROWS, HEAD), F32)],
        compiler_params=pltpu.CompilerParams(vmem_limit_bytes=VMEM_BYTES),
        cost_estimate=pl.CostEstimate(flops=10000000000, bytes_accessed=1000000, transcendentals=0),
    )(slots, parts)


def down_kernel(slots, parts, out):
    for s in range(16):
        rows = take_down(parts.at[slots[s]], 0).astype(F32)
        out[s * BLOCK : (s + 1) * BLOCK, :] = rows[:BLOCK]


def down_out(slots, parts):
    below = SEND_ROWS - ROWS
    return pl.pallas_call(
        down_kernel,
        grid_spec=pltpu.PrefetchScalarGridSpec(
            num_scalar_prefetch=1,
            grid=(1,),
            in_specs=[pl.BlockSpec((NCTX, below, WIDE), lambda i, s: (0, ROWS // below, 0))],
            out_specs=pl.BlockSpec((FF // NFS, D), lambda i, s: (0, 0)),
        ),
        out_shape=sds((FF // NFS, D), F32),
        compiler_params=pltpu.CompilerParams(vmem_limit_bytes=VMEM_BYTES),
        cost_estimate=pl.CostEstimate(flops=7000000000, bytes_accessed=1000000, transcendentals=0),
    )(slots, parts)


def angle_tables():
    freqs = THETA ** (-(np.arange(HEAD // 2) * 2.0 / HEAD))
    angle = np.arange(SEQ)[:, None] * np.concatenate([freqs, freqs])[None, :]
    turn = np.where(np.arange(HEAD) < HEAD // 2, -1.0, 1.0)[None, :]
    return jnp.asarray(np.cos(angle), F32), jnp.asarray(np.sin(angle) * turn, F32)


def on_device(
    inputs,
    segments,
    gain_attn,
    w_query,
    b_query,
    w_key,
    b_key,
    w_value,
    b_value,
    w_output,
    gain_mlp,
    w_gate,
    w_up,
    w_down,
    cotangent,
):
    c, f = lax.axis_index("context"), lax.axis_index("fsdp")
    x, yl, core, z, yh = split_place(c, f)
    rel_ctx = jnp.stack([((x + a) % 4) * 4 + (yl ^ b) * 2 + (core ^ k) for k in range(2) for a, b in REL8])
    rel_ctx = rel_ctx.astype(jnp.int32)
    rel_shard = [((z + a) % 4) * 2 + (yh ^ b) for a, b in REL8]
    meta = jnp.stack([core, c // 2, *rel_shard]).astype(jnp.int32)
    rel_line = meta[2:10]
    cosine, sine = angle_tables()
    gain_one = gain_attn.astype(F32)[:, None]
    gain_two = gain_mlp.astype(F32)[:, None]
    tokens, cot = inputs[0], cotangent[0]

    unit, piece = call(
        first_kernel,
        [sds((TOK + 16, D)), sds((ROWS + 16, PART + HALF))],
        [SCALARS] + [WHOLE] * 10,
        3,
        scratch_shapes=[pltpu.VMEM((8, D), F32), pltpu.VMEM((8, 256), F32)],
    )(
        jnp.stack([f, core]).astype(jnp.int32),
        tokens,
        segments,
        w_query,
        w_key,
        w_value,
        w_output,
        gain_one,
        b_query.astype(F32)[None],
        b_key.astype(F32)[None],
        b_value.astype(F32)[None],
    )
    mlp_piece, gu_own = call(
        slice_kernel,
        [sds((SEND_ROWS, WIDE)), sds((ROWS, WIDE))],
        [SCALARS] + [WHOLE] * 4,
        6,
        scratch_shapes=[pltpu.VMEM((ROWS, WIDE), F32)],
    )((c ^ (2 * yh))[None].astype(jnp.int32), w_gate, w_up, w_down, gain_two)
    got, _ = together(gather_one(piece, SLICES) + [(unit, "core")])
    one, unit_other = got[:3], got[3]
    cots = lax.all_gather(after(cot, *got), "context", axis=0, tiled=True)
    two, (mlp_piece, gu_own) = together([(one[2], "z+"), (one[1], "z-")], mlp_piece, gu_own)
    got, _ = together([(one[2], "z-"), (two[0], "z+"), (mlp_piece, "yw")])
    two, three, m_pair = [*two, got[0]], got[1:2], got[2]

    q, kv, w_part, units = call(
        project_kernel,
        [sds((GROUP * CHIP, HEAD)), sds((8, CHIP + 16, 2 * HEAD)), sds((D, PART)), sds((CHIP, D))],
        [SCALARS] + [WHOLE] * 12,
        5,
    )(meta, unit, unit_other, piece, *one, *two, *three, cosine, sine)
    all_kv = over_chips(kv)
    m_one = [send(after(mlp_piece, kv), "z+"), send(after(mlp_piece, kv), "z-")]

    rows = sds((GROUP * CHIP, HEAD), F32)
    att, wide, lse, k, v, cuts = call(
        fwd_kernel,
        [sds((CHIP, HALF)), rows, rows, sds((SEQ, HEAD)), sds((SEQ, HEAD)), sds((2,), jnp.int32)],
        [SCALARS] + [WHOLE] * 2,
        20,
        out_specs=[WHOLE] * 5 + [SCALARS],
        scratch_shapes=[pltpu.VMEM((GROUP * CHIP, HEAD), F32)] * 3,
    )(meta, q, all_kv)

    _, (att, *m_one) = together([], att, *m_one)
    m_one = [*m_one, m_pair]
    m_two = [send(value, move) for value, move in gather_two(m_one, SLICES)]
    (att_other,), _ = together([(att, "core")])
    res_mine, res_theirs, atts, wo_turned = call(
        out_kernel,
        [sds((TOK, HALF), F32), sds((TOK, HALF), F32), sds((CHIP, D)), sds((HALF, D))],
        [SCALARS] + [WHOLE] * 10,
        4,
        scratch_shapes=[pltpu.VMEM((D, HALF), BF), pltpu.VMEM((CHIP, HALF), F32)],
    )(meta, att, att_other, piece, *one, *two, *three)
    (res_got,), _ = together([(res_theirs, "core")])
    residual, unit_two = call(
        residual_kernel, [sds((TOK, D), F32), sds((TOK, D))], [SCALARS] + [WHOLE] * 3, 2
    )(meta, tokens, res_mine, res_got)
    _, (unit_two, cots, *m_two) = together([], unit_two, cots, *m_two)

    got, _ = together(gather_one(unit_two, CTX) + gather_three(m_two, SLICES) + [(unit_two, "core")])
    one, m_three, other = got[:3], got[3:4], got[4:]
    got, _ = together(gather_two(one, CTX) + [(p, "core") for p in one])
    two, other = got[:3], other + got[3:6]
    w, w_turned, w_d, w_part_turned = call(
        weights_kernel,
        [sds((D, 3 * SLOT)), sds((2 * SLOT, D)), sds((SLOT, D)), sds((PART, D))],
        [SCALARS] + [WHOLE] * 9,
        10,
    )(rel_line, mlp_piece, *m_one, *m_two, *m_three, w_part)
    got, (w, w_turned) = together(gather_three(two, CTX) + [(p, "core") for p in two], w, w_turned)
    three, other = got[:1], other + got[1:4]
    twos = [unit_two, *one, *two, *three, *other, send(three[0], "core")]

    u2, hidden, grad_gate, grad_up, gnt_mine, gnt_other = mlp(rel_ctx, twos, cots, w, w_turned)

    got, _ = together([(gnt_other, "core")])
    q_two = pair_sum(gnt_mine, got[0])
    dw_gate = times_first(after(u2, *got), grad_gate).astype(BF)
    one, (dw_gate,) = together(sum_one(q_two, CTX), dw_gate)
    dw_up = times_first(u2, after(grad_up, *one)).astype(BF)
    two, (dw_up,) = together(sum_two(q_two, one, CTX), dw_up)
    dw_d = times_first(after(hidden, *two), cots).astype(BF)
    dealt = call(deal_kernel, [sds((SEND_ROWS, WIDE))] * 8, [SCALARS] + [WHOLE] * 3, 5)(
        rel_line, dw_gate, dw_up, dw_d
    )
    three, dealt = together(sum_three(q_two, one, two, CTX), *dealt)
    q_mlp = dealt.__getitem__

    s_one = [send(value, move) for value, move in sum_one(q_mlp, SLICES)]
    grad_residual, gao_mine, gao_theirs = call(
        norm_two_kernel,
        [sds((TOK, D), F32), sds((TOK, HALF)), sds((TOK, HALF))],
        [SCALARS] + [WHOLE] * 6,
        2,
        scratch_shapes=[pltpu.VMEM((TOK, D), BF)],
    )(meta, q_two(0), two[2], three[0], three[1], residual, cot)
    (gao_got,), _ = together([(gao_theirs, "core")])
    ga_mine, ga_theirs, gaos = call(
        out_grad_kernel,
        [sds((CHIP, HALF), F32), sds((CHIP, HALF)), sds((CHIP, HALF))],
        [SCALARS] + [WHOLE] * 3,
        3,
        scratch_shapes=[pltpu.VMEM((CHIP, D), F32)],
    )(meta, gao_mine, gao_got, wo_turned)
    (ga_got,), _ = together([(ga_theirs, "core")])

    stacked = pltpu.VMEM((GROUP * CHIP, HEAD), F32)
    dq, dkv = call(
        bwd_kernel,
        [sds((CHIP, HALF)), sds((SEQ, 2 * HEAD))],
        [SCALARS] * 2 + [WHOLE] * 9,
        28,
        scratch_shapes=[
            pltpu.VMEM((GROUP * CHIP, HEAD), BF),
            stacked,
            pltpu.VMEM((GROUP * CHIP, BK), BF),
            pltpu.VMEM((GROUP * CHIP, BK), BF),
            stacked,
            pltpu.VMEM((SEQ, HEAD), F32),
            pltpu.VMEM((SEQ, HEAD), F32),
        ],
    )(meta, cuts, q, k, v, wide, lse, cosine, sine, ga_mine, ga_got)
    _, (dq, dkv, *s_one) = together([], dq, dkv, *s_one)
    s_two = [send(value, move) for value, move in sum_two(q_mlp, s_one, SLICES)]

    all_dkv = over_chips(dkv)
    down_mine, down_other = through_down(rel_ctx, after(hidden, dkv), w_d)
    _, (all_dkv, down_mine, down_other, *s_two) = together([], all_dkv, down_mine, down_other, *s_two)
    s_three = [send(value, move) for value, move in sum_three(q_mlp, s_one, s_two, SLICES)]
    down_got = send(down_other, "core")

    gu1_mine, gu1_theirs, *pieces = call(
        project_grad_kernel,
        [sds((TOK, D), F32), sds((TOK, D))] + [sds((ROWS + 16, PART + HALF))] * 8,
        [SCALARS] + [WHOLE] * 8,
        9,
        scratch_shapes=[pltpu.VMEM((CHIP, PART), BF), pltpu.VMEM((D, PART + HALF), BF), pltpu.VMEM((CHIP, D), F32)],
    )(meta, all_dkv, dq, units, w_part_turned, cosine, sine, atts, gaos)

    _, (down_got, *pieces) = together([], down_got, *pieces)
    q_attn, q_down = pieces.__getitem__, pair_sum(down_mine, down_got)
    mine = call(slice_sum_kernel, sds((SEND_ROWS, WIDE)), [WHOLE] * 6, 3)(
        q_mlp(0), s_two[2], *s_three, gu_own, gain_two
    )
    got, (mine,) = together(sum_one(q_attn, SLICES) + [(gu1_theirs, "core")] + sum_one(q_down, CTX), mine)
    a_one, d_one = got[:2], got[3:]
    mlp_grads = lax.all_gather(mine, "context", axis=0)
    grad_tokens = call(norm_one_kernel, sds((TOK, D)), [WHOLE] * 4, 2)(gu1_mine, got[2], tokens, grad_residual)
    a_two, (grad_tokens,) = together(sum_two(q_attn, a_one, SLICES), grad_tokens)
    got, _ = together(sum_three(q_attn, a_one, a_two, SLICES) + sum_two(q_down, d_one, CTX))
    a_three, d_two = got[:2], got[2:]

    dealt = call(
        line_deal_kernel,
        sds((8, ROWS + 16, 2 * HEAD)),
        [WHOLE] * 4,
        3,
        scratch_shapes=[pltpu.VMEM((ROWS + 16, PART + HALF), F32)],
    )(q_attn(0), a_two[2], *a_three)
    blocks = over_chips(dealt)
    slots = jnp.arange(NCTX, dtype=jnp.int32) ^ (2 * yh)
    _, (blocks,) = together([], blocks)
    block = call(block_kernel, sds((8, ROWS + 16, 2 * HEAD)), [SCALARS] + [WHOLE] * 5, 2)(
        meta, blocks, w_query, w_key, w_value, gain_one
    )

    attn_mine = over_chips(block)
    grad_gate_w, grad_up_w, gain_two_cols = gate_up_out(slots, after(mlp_grads, block))
    grad_down_w = down_out(slots, after(mlp_grads, block))
    d_three = [send(after(value, block), move) for value, move in sum_three(q_down, d_one, d_two, CTX)]
    output = (residual + sum_all(q_down, d_two, d_three)).astype(BF)
    _, (attn_mine, grad_gate_w, grad_down_w) = together([], attn_mine, grad_gate_w, grad_down_w)
    attn_other = send(attn_mine, "core")

    grad_wq, grad_wk, grad_wv, grad_wo, sum_bq, sum_bk, sum_bv, grad_gain_one = call(
        attn_kernel,
        [
            sds((ROWS, D), F32),
            sds((ROWS, 256), F32),
            sds((ROWS, 256), F32),
            sds((ROWS, D), F32),
            sds((1, ROWS), F32),
            sds((1, 32), F32),
            sds((1, 32), F32),
            sds((1, ROWS), F32),
        ],
        [SCALARS, WHOLE, WHOLE],
        4,
        scratch_shapes=[
            pltpu.VMEM((8, D), F32),
            pltpu.VMEM((2, 8, 256), F32),
        ],
    )(jnp.stack([f, core]).astype(jnp.int32), attn_mine, attn_other)
    return (
        output[None],
        grad_tokens[None],
        grad_gain_one[0],
        grad_wq,
        sum_bq[0],
        grad_wk,
        sum_bk[0],
        grad_wv,
        sum_bv[0],
        grad_wo,
        gain_two_cols[:, HEAD - 1],
        grad_gate_w,
        grad_up_w,
        grad_down_w,
    )


def solution(mesh):
    tokens = P("fsdp", "context", None)
    matrix, vector = P("fsdp", None), P("fsdp")
    weights = (vector, matrix, vector, matrix, vector, matrix, vector, matrix, vector, matrix, matrix, matrix)
    return jax.shard_map(
        on_device,
        mesh=mesh,
        in_specs=(tokens, P("fsdp", "context"), *weights, tokens),
        out_specs=(tokens, tokens, *weights),
        check_vma=False,
    )
```

```python
import math

import jax
import jax.numpy as jnp
import numpy as np
from jax import lax
from jax.experimental import pallas as pl
from jax.experimental.pallas import tpu as pltpu
from jax.sharding import PartitionSpec as P

D = 1536
FF = 8960
HEADS = 12
KV_HEADS = 2
HEAD = 128
GROUP = HEADS // KV_HEADS
HALF = D // 2
PART = HALF + 2 * HEAD
SEQ = 2048
EPS = 1e-06
THETA = 1000000.0
NCTX, NFS = 16, 8
TOK = SEQ // NCTX
ROWS = D // NFS
BLOCK = FF // NFS // NCTX
PIECE = 80
SLOT = NFS * PIECE
SEND_ROWS = ROWS + PIECE + 16
AXES = ("context", "fsdp")
SCALE = 1.0 / math.sqrt(HEAD)
LOG2E = math.log2(math.e)
CHIP = 256
BK = 1024
BF, F32 = jnp.bfloat16, jnp.float32
VMEM_BYTES = 58 * 1024 * 1024
NEG = -1e30


def split_place(c, f):
    return c // 4, (c // 2) % 2, c % 2, f // 2, f % 2


def pairs_of(move):
    pairs = []
    for c in range(NCTX):
        for f in range(NFS):
            x, yl, core, z, yh = move(*split_place(c, f))
            pairs.append((c * NFS + f, ((x % 4) * 4 + (yl % 2) * 2 + core % 2) * NFS + (z % 4) * 2 + yh % 2))
    return pairs


MOVES = {
    "x+": pairs_of(lambda x, yl, core, z, yh: (x + 1, yl, core, z, yh)),
    "x-": pairs_of(lambda x, yl, core, z, yh: (x - 1, yl, core, z, yh)),
    "yl": pairs_of(lambda x, yl, core, z, yh: (x, yl + 1, core, z, yh)),
    "core": pairs_of(lambda x, yl, core, z, yh: (x, yl, core + 1, z, yh)),
    "z+": pairs_of(lambda x, yl, core, z, yh: (x, yl, core, z + 1, yh)),
    "z-": pairs_of(lambda x, yl, core, z, yh: (x, yl, core, z - 1, yh)),
    "yw": pairs_of(lambda x, yl, core, z, yh: (x, yl + 1, core, z, yh + 1)),
}
SAME_CORE = [[c for c in range(NCTX) if c % 2 == core] for core in range(2)]


def send(value, move):
    pairs = MOVES[move] if isinstance(move, str) else move
    return lax.ppermute(value, AXES, pairs)


def add(*terms):
    total = terms[0].astype(F32)
    for t in terms[1:]:
        total = total + t.astype(F32)
    return total


def after(value, *earlier):
    return lax.optimization_barrier((value, *earlier))[0]


def together(sends, *rest):
    got = [send(value, move) for value, move in sends]
    done = lax.optimization_barrier((*got, *rest))
    return list(done[: len(got)]), list(done[len(got) :])


REL8 = [(0, 0), (-1, 0), (1, 0), (0, 1), (-1, 1), (2, 0), (1, 1), (2, 1)]
CTX, SLICES = ("x+", "x-", "yl"), ("z+", "z-", "yw")


def over_chips(terms):
    return lax.all_to_all(terms, "context", 0, 0, axis_index_groups=SAME_CORE, tiled=True)


def gather_one(v, way):
    return [(v, way[0]), (v, way[1]), (v, way[2])]


def gather_two(parts, way):
    _, b, c = parts
    return [(c, way[0]), (b, way[1]), (b, way[2])]


def gather_three(parts, way):
    return [(parts[1], way[2])]


def sum_one(q, way):
    return [(q(7), way[2]), (q(4), way[1])]


def sum_two(q, got, way):
    later = [after(q(j), *got[:2]) for j in (6, 1)]
    return [(add(q(5), got[0]).astype(BF), way[0]), (later[0], way[2]), (later[1], way[1])]


def sum_three(q, one, two, way):
    return [(add(q(2), two[0], two[1]).astype(BF), way[0]), (add(q(3), one[1]).astype(BF), way[2])]


def sum_all(q, two, three):
    return add(q(0), two[2], three[0], three[1])


def pair_sum(mine, other):
    n = mine.shape[0] // 8
    return lambda j: add(mine[j * n : (j + 1) * n], other[j * n : (j + 1) * n]).astype(BF)


def times_last(left, right):
    return lax.dot_general(left, right, (((1,), (1,)), ((), ())), preferred_element_type=F32)


def times_first(left, right):
    return lax.dot_general(left, right, (((0,), (0,)), ((), ())), preferred_element_type=F32)


def dot(left, right):
    return jnp.dot(left, right, preferred_element_type=F32)


def sds(shape, dtype=BF):
    return jax.ShapeDtypeStruct(shape, dtype)


WHOLE = pl.BlockSpec(memory_space=pltpu.VMEM)
SCALARS = pl.BlockSpec(memory_space=pltpu.SMEM)
ANYWHERE = pl.BlockSpec(memory_space=pl.ANY)


def call(kernel, out_shape, specs, us, **kw):
    return pl.pallas_call(
        kernel,
        out_shape=out_shape,
        in_specs=specs,
        compiler_params=pltpu.CompilerParams(vmem_limit_bytes=VMEM_BYTES),
        cost_estimate=pl.CostEstimate(flops=int(us * 1.0e9), bytes_accessed=int(us * 1e5), transcendentals=0),
        **kw,
    )


def first_kernel(
    at, tokens, ids, w_query, w_key, w_value, w_out, gain, b_query, b_key, b_value, unit, piece, wide, narrow
):
    f, core = at[0], at[1]
    x = tokens[...].astype(F32)
    unit[:TOK, :] = (x * lax.rsqrt(jnp.mean(x * x, axis=1, keepdims=True) + EPS)).astype(BF)
    lane = lax.broadcasted_iota(jnp.int32, (16, D), 1)
    before = [jnp.sum((ids[...] < n).astype(F32), axis=1, keepdims=True) for n in (1, 2)]
    unit[TOK:, :] = jnp.where(lane == 0, before[0], jnp.where(lane == 1, before[1], 0.0)).astype(BF)
    scale = gain[...]
    qs = pl.ds(pl.multiple_of(core * HALF, HALF), HALF)
    ks = pl.ds(pl.multiple_of(core * HEAD, HEAD), HEAD)
    piece[:ROWS, :HALF] = (w_query[:, qs].astype(F32) * scale).astype(BF)
    piece[:ROWS, HALF : HALF + HEAD] = (w_key[:, ks].astype(F32) * scale).astype(BF)
    piece[:ROWS, PART:] = w_out[:, qs]
    piece[:ROWS, HALF + HEAD : PART] = (w_value[:, ks].astype(F32) * scale).astype(BF)
    piece[ROWS:, :] = jnp.zeros((16, PART + HALF), BF)
    wide[...] = jnp.zeros_like(wide)
    wide[0:1, :ROWS] = b_query[...]
    wide[...] = pltpu.roll(wide[...], f * ROWS, 1)
    piece[ROWS : ROWS + 8, :HALF] = wide[:, qs].astype(BF)
    for b, at_col in ((b_key, HALF), (b_value, HALF + HEAD)):
        narrow[...] = jnp.zeros_like(narrow)
        narrow[0:1, :32] = b[...]
        narrow[...] = pltpu.roll(narrow[...], f * 32, 1)
        piece[ROWS : ROWS + 8, at_col : at_col + HEAD] = narrow[:, ks].astype(BF)


def both_cores(core, mine, theirs, out):
    n = mine.shape[0]
    out[pl.ds(pl.multiple_of(core * n, n), n), :] = mine
    out[pl.ds(pl.multiple_of((1 - core) * n, n), n), :] = theirs


def rotated(y, cosine, sine):
    return y * cosine + pltpu.roll(y, HEAD // 2, 1) * sine


def project_kernel(meta, unit, unit_other, *refs):
    parts, (cosine, sine, q, kv, w, units) = refs[:8], refs[8:]
    core, chip = meta[0], meta[1]
    both_cores(core, unit[:TOK, :], unit_other[:TOK, :], units)
    bias = jnp.zeros((1, PART), F32)
    for j in range(8):
        w[pl.ds(pl.multiple_of(meta[2 + j] * ROWS, ROWS), ROWS), :] = parts[j][:ROWS, :PART]
        bias += parts[j][ROWS:, :PART].astype(F32)[:1]
    y = dot(units[...], w[...]) + bias
    here = pl.ds(pl.multiple_of(chip * CHIP, CHIP), CHIP)
    cos_rows, sin_rows = cosine[here, :], sine[here, :]
    for h in range(GROUP):
        turned = rotated(y[:, h * HEAD : (h + 1) * HEAD], cos_rows, sin_rows)
        q[h * CHIP : (h + 1) * CHIP, :] = (turned * (SCALE * LOG2E)).astype(BF)
    keys = rotated(y[:, HALF : HALF + HEAD], cos_rows, sin_rows).astype(BF)
    vals = y[:, HALF + HEAD :].astype(BF)
    counts = unit[TOK:, : 2 * HEAD].astype(F32) + unit_other[TOK:, : 2 * HEAD].astype(F32)
    for to in range(8):
        kv[to, :CHIP, :HEAD] = keys
        kv[to, :CHIP, HEAD:] = vals
        kv[to, CHIP:, :] = counts.astype(BF)


def doc_begins(cuts, places):
    return jnp.where(places < cuts[0], 0, jnp.where(places < cuts[1], cuts[0], cuts[1]))


def visible_keys(cuts, chip, kb):
    places = chip * CHIP + lax.broadcasted_iota(jnp.int32, (CHIP, 1), 0)
    keys = kb * BK + lax.broadcasted_iota(jnp.int32, (1, BK), 1)
    return (keys <= places) & (keys >= doc_begins(cuts, places))


def key_blocks(cuts, chip):
    return doc_begins(cuts, chip * CHIP) // BK, chip // (BK // CHIP) + 1


def fwd_kernel(meta, q, *refs):
    parts, out, wide, lse, k, v, cuts_out, top, total, acc = refs
    chip = meta[1]
    lane = lax.broadcasted_iota(jnp.int32, (1, HEAD), 1)
    counts = sum(parts[j, CHIP:, :HEAD].astype(F32) for j in range(8))[:1]
    cuts = [jnp.sum(jnp.where(lane == i, counts, 0.0)).astype(jnp.int32) for i in range(2)]
    cuts_out[0], cuts_out[1] = cuts
    for j in range(8):
        there = slice(j * CHIP, (j + 1) * CHIP)
        k[there, :] = parts[j, :CHIP, :HEAD]
        v[there, :] = parts[j, :CHIP, HEAD:]
    top[...] = jnp.full_like(top, NEG)
    total[...] = jnp.zeros_like(total)
    acc[...] = jnp.zeros_like(acc)

    def step(kb, _):
        there = pl.ds(pl.multiple_of(kb * BK, BK), BK)
        keys, vals = k[there, :], v[there, :]
        visible = visible_keys(cuts, chip, kb)
        for h in range(GROUP):
            rows = slice(h * CHIP, (h + 1) * CHIP)
            s = jnp.where(visible, times_last(q[rows, :], keys), NEG)
            old = top[rows, :]
            new = jnp.maximum(old, jnp.max(s, axis=1, keepdims=True))
            p = jnp.exp2(s - new[:, :1])
            fade = jnp.exp2(old - new)
            top[rows, :] = new
            total[rows, :] = total[rows, :] * fade + jnp.sum(p, axis=1, keepdims=True)
            acc[rows, :] = acc[rows, :] * fade + dot(p.astype(BF), vals)
        return 0

    lo, hi = key_blocks(cuts, chip)
    lax.fori_loop(lo, hi, step, 0)
    for h in range(GROUP):
        rows, cols = slice(h * CHIP, (h + 1) * CHIP), slice(h * HEAD, (h + 1) * HEAD)
        result = acc[rows, :] / total[rows, :]
        out[:, cols] = result.astype(BF)
        wide[rows, :] = result
        lse[rows, :] = top[rows, :] + jnp.log2(total[rows, :])


def bwd_kernel(meta, cuts_in, q, k, v, wide, lse, cosine, sine, grad, grad_other, dq_out, dkv, go, delta, p_all, ds_all, dq, dk, dv):
    core, chip = meta[0], meta[1]
    cuts = (cuts_in[0], cuts_in[1])
    dq[...] = jnp.zeros_like(dq)
    dk[...] = jnp.zeros_like(dk)
    dv[...] = jnp.zeros_like(dv)
    for h in range(GROUP):
        rows, cols = slice(h * CHIP, (h + 1) * CHIP), slice(h * HEAD, (h + 1) * HEAD)
        low = (grad[:, cols] + grad_other[:, cols].astype(F32)).astype(BF)
        go[rows, :] = low
        found = jnp.sum(low.astype(F32) * wide[rows, :], axis=1, keepdims=True)
        delta[rows, :] = jnp.broadcast_to(found, (CHIP, HEAD))

    def step(kb, _):
        there = pl.ds(pl.multiple_of(kb * BK, BK), BK)
        keys, vals = k[there, :], v[there, :]
        visible = visible_keys(cuts, chip, kb)
        for h in range(GROUP):
            rows = slice(h * CHIP, (h + 1) * CHIP)
            s = jnp.where(visible, times_last(q[rows, :], keys), NEG)
            p = jnp.exp2(s - lse[rows, :1])
            dp = times_last(go[rows, :], vals)
            ds = (p * (dp - delta[rows, :1])).astype(BF)
            p_all[rows, :] = p.astype(BF)
            ds_all[rows, :] = ds
            dq[rows, :] += dot(ds, keys)
        dv[there, :] = times_first(p_all[...], go[...])
        dk[there, :] = times_first(ds_all[...], q[...])
        return 0

    lo, hi = key_blocks(cuts, chip)
    lax.fori_loop(lo, hi, step, 0)
    here = pl.ds(pl.multiple_of(chip * CHIP, CHIP), CHIP)
    cos_rows, sin_rows = cosine[here, :], -sine[here, :]
    for h in range(GROUP):
        rows, cols = slice(h * CHIP, (h + 1) * CHIP), slice(h * HEAD, (h + 1) * HEAD)
        dq_out[:, cols] = rotated(dq[rows, :] * SCALE, cos_rows, sin_rows).astype(BF)
    dkv[:, :HEAD] = (dk[...] * (1.0 / LOG2E)).astype(BF)
    dkv[:, HEAD:] = dv[...].astype(BF)


def out_kernel(meta, att, att_other, *refs):
    parts, (mine, theirs, atts, w_turned, w, held) = refs[:8], refs[8:]
    core = meta[0]
    atts[:, pl.ds(pl.multiple_of(core * HALF, HALF), HALF)] = att[...]
    atts[:, pl.ds(pl.multiple_of((1 - core) * HALF, HALF), HALF)] = att_other[...]
    for j in range(8):
        w[pl.ds(pl.multiple_of(meta[2 + j] * ROWS, ROWS), ROWS), :] = parts[j][:ROWS, PART:]
    held[...] = dot(atts[...], w[...])
    mine[...] = held[pl.ds(pl.multiple_of(core * TOK, TOK), TOK), :]
    theirs[...] = held[pl.ds(pl.multiple_of((1 - core) * TOK, TOK), TOK), :]
    for i in range(HALF // 256):
        cols = slice(i * 256, (i + 1) * 256)
        w_turned[cols, :] = jnp.transpose(w[:, cols])


def residual_kernel(meta, tokens, mine, got, residual, unit):
    core = meta[0]
    here = pl.ds(pl.multiple_of(core * HALF, HALF), HALF)
    there = pl.ds(pl.multiple_of((1 - core) * HALF, HALF), HALF)
    residual[:, here] = tokens[:, here].astype(F32) + mine[...]
    residual[:, there] = tokens[:, there].astype(F32) + got[...]
    x = residual[...]
    unit[...] = (x * lax.rsqrt(jnp.mean(x * x, axis=1, keepdims=True) + EPS)).astype(BF)


def norm_grad(x, grad):
    scale = lax.rsqrt(jnp.mean(x * x, axis=1, keepdims=True) + EPS)
    unit = x * scale
    return scale * (grad - unit * jnp.mean(grad * unit, axis=1, keepdims=True))


def norm_two_kernel(meta, term, a, b, c, residual, cot, grad_residual, mine, theirs, held):
    core = meta[0]
    grad = add(term[...], a[...], b[...], c[...])
    result = cot[...].astype(F32) + norm_grad(residual[...], grad)
    grad_residual[...] = result
    held[...] = result.astype(BF)
    mine[...] = held[:, pl.ds(pl.multiple_of(core * HALF, HALF), HALF)]
    theirs[...] = held[:, pl.ds(pl.multiple_of((1 - core) * HALF, HALF), HALF)]


def out_grad_kernel(meta, grad, grad_other, w_turned, mine, theirs, grads, held):
    core = meta[0]
    both_cores(core, grad[...], grad_other[...], grads)
    held[...] = dot(grads[...], w_turned[...])
    mine[...] = held[:, pl.ds(pl.multiple_of(core * HALF, HALF), HALF)]
    theirs[...] = held[:, pl.ds(pl.multiple_of((1 - core) * HALF, HALF), HALF)].astype(BF)


def project_grad_kernel(meta, terms, dq, units, w_turned, cosine, sine, atts, grads, mine, theirs, *refs):
    pieces, (both, dw, held) = refs[:8], refs[8:]
    core, chip = meta[0], meta[1]
    here = pl.ds(pl.multiple_of(chip * CHIP, CHIP), CHIP)
    dkv = add(*[terms[j * CHIP : (j + 1) * CHIP, :] for j in range(8)])
    both[:, :HALF] = dq[...]
    both[:, HALF : HALF + HEAD] = rotated(dkv[:, :HEAD], cosine[here, :], -sine[here, :]).astype(BF)
    both[:, HALF + HEAD :] = dkv[:, HEAD:].astype(BF)
    held[...] = dot(both[...], w_turned[...])
    mine[...] = held[pl.ds(pl.multiple_of(core * TOK, TOK), TOK), :]
    theirs[...] = held[pl.ds(pl.multiple_of((1 - core) * TOK, TOK), TOK), :].astype(BF)
    dw[:, :PART] = times_first(units[...], both[...]).astype(BF)
    dw[:, PART:] = times_first(atts[...], grads[...]).astype(BF)
    bias = jnp.sum(both[...].astype(F32), axis=0, keepdims=True)
    bias = jnp.broadcast_to(bias, (16, PART)).astype(BF)
    for j, out in enumerate(pieces):
        out[:ROWS, :] = dw[pl.ds(pl.multiple_of(meta[2 + j] * ROWS, ROWS), ROWS), :]
        out[ROWS:, :PART] = bias
        out[ROWS:, PART:] = jnp.zeros((16, HALF), BF)


def norm_one_kernel(mine, got, tokens, grad_residual, out):
    grad = mine[...] + got[...].astype(F32)
    out[...] = (grad_residual[...] + norm_grad(tokens[...].astype(F32), grad)).astype(BF)


def line_deal_kernel(term, a, b, c, *refs):
    out, total = refs
    total[...] = add(term[...], a[...], b[...], c[...])
    for chip in range(8):
        out[chip, :, :HEAD] = total[:, chip * HEAD : (chip + 1) * HEAD].astype(BF)
        at = PART + min(chip, GROUP - 1) * HEAD
        out[chip, :, HEAD:] = total[:, at : at + HEAD].astype(BF)


def block_kernel(meta, terms, w_query, w_key, w_value, gain, out):
    core, chip = meta[0], meta[1]
    total = add(*[terms[j] for j in range(8)])
    head = core * GROUP + jnp.minimum(chip, GROUP - 1)
    wq = w_query[:, pl.ds(pl.multiple_of(head * HEAD, HEAD), HEAD)].astype(F32)
    ks = pl.ds(pl.multiple_of(core * HEAD, HEAD), HEAD)
    wk, wv = w_key[:, ks].astype(F32), w_value[:, ks].astype(F32)
    w = jnp.where(chip < GROUP, wq, jnp.where(chip == GROUP, wk, wv))
    grad = total[:ROWS, :HEAD]
    for_gain = jnp.sum(grad * w, axis=1, keepdims=True)
    for_gain = jnp.transpose(jnp.broadcast_to(for_gain, (ROWS, HEAD)))
    low = (grad * gain[...]).astype(BF)
    beside = total[:ROWS, HEAD:].astype(BF)
    row = lax.broadcasted_iota(jnp.int32, (16, 2 * HEAD), 0)
    gains = jnp.concatenate([for_gain[:16, :], jnp.zeros((16, 2 * HEAD - ROWS), F32)], axis=1)
    below = jnp.where(row == 0, total[ROWS:, :], gains).astype(BF)
    for to in range(8):
        out[to, :ROWS, :HEAD] = low
        out[to, :ROWS, HEAD:] = beside
        out[to, ROWS:, :] = below


def attn_kernel(slots, *refs):
    held, wq, wk, wv, wo, bq, bk, bv, gain, wide, narrow = refs[0:2], *refs[2:]
    f, mine = slots[0], slots[1]
    total = jnp.zeros((16, 2 * HEAD), F32)
    for core in range(2):
        cols = slice(core * HEAD, (core + 1) * HEAD)
        for chip in range(8):
            block = jnp.where(mine == core, held[0][chip], held[1][chip]).astype(F32)
            total += block[ROWS:, :]
            if chip < GROUP:
                at = slice((core * GROUP + chip) * HEAD, (core * GROUP + chip + 1) * HEAD)
                wq[:, at] = block[:ROWS, :HEAD]
                wo[:, at] = block[:ROWS, HEAD:]
                wide[:, at] = block[ROWS : ROWS + 8, :HEAD]
            else:
                out, i = ((wk, 0), (wv, 1))[chip - GROUP]
                out[:, cols] = block[:ROWS, :HEAD]
                narrow[i, :, cols] = block[ROWS : ROWS + 8, :HEAD]
    gain[...] = total[1:2, :ROWS]
    bq[...] = pltpu.roll(wide[...], D - f * ROWS, 1)[:1, :ROWS]
    bk[...] = pltpu.roll(narrow[0], 256 - f * 32, 1)[:1, :32]
    bv[...] = pltpu.roll(narrow[1], 256 - f * 32, 1)[:1, :32]


WIDE = 2 * SLOT
TAIL = D - WIDE


def slice_kernel(at, w_gate, w_up, w_down, gain, out, own, gathered):
    lane = lax.broadcasted_iota(jnp.int32, (ROWS, PIECE), 1)
    for i, w in enumerate((w_gate, w_up)):
        for j in range(NFS):
            start = j * (FF // NFS) + at[0] * BLOCK
            base = jnp.minimum(start // 128 * 128, FF - 256)
            window = w[:, pl.ds(pl.multiple_of(base, 128), 256)].astype(F32)
            window = pltpu.roll(window, 256 - (start - base), 1)[:, :PIECE]
            gathered[:, i * SLOT + j * PIECE : i * SLOT + (j + 1) * PIECE] = jnp.where(lane < BLOCK, window, 0.0)
    own[...] = gathered[...].astype(BF)
    out[:ROWS, :] = (gathered[...] * gain[...]).astype(BF)
    start = at[0] * BLOCK
    base = jnp.minimum(start // 16 * 16, FF // NFS - 96)
    window = w_down[pl.ds(pl.multiple_of(base, 16), 96), :].astype(F32)
    window = pltpu.roll(window, 96 - (start - base), 0)[:PIECE]
    row = lax.broadcasted_iota(jnp.int32, (PIECE, D), 0)
    put_down(out, jnp.where(row < BLOCK, window, 0.0).astype(BF))


def put_down(out, rows):
    out[ROWS : ROWS + PIECE, :] = rows[:, :WIDE]
    for i in range(PIECE // 16):
        out[ROWS + PIECE :, i * TAIL : (i + 1) * TAIL] = rows[i * 16 : (i + 1) * 16, WIDE:]


def take_down(part, at):
    tail = [part[at + PIECE :, i * TAIL : (i + 1) * TAIL] for i in range(PIECE // 16)]
    return jnp.concatenate([part[at : at + PIECE, :], jnp.concatenate(tail, axis=0)], axis=1)


def weights_kernel(order, *refs):
    parts, qkv = refs[:8], refs[8]
    w, w_turned, down, qkv_turned = refs[9:]
    for j in range(8):
        w[pl.ds(pl.multiple_of(order[j] * ROWS, ROWS), ROWS), :WIDE] = parts[j][:ROWS, :]
        down[pl.ds(pl.multiple_of(order[j] * PIECE, 16), PIECE), :] = take_down(parts[j], ROWS)
    for i in range(WIDE // 256):
        w_turned[i * 256 : (i + 1) * 256, :] = jnp.transpose(w[:, i * 256 : (i + 1) * 256])
    for i in range(SLOT // 128):
        w[:, WIDE + i * 128 : WIDE + (i + 1) * 128] = jnp.transpose(down[i * 128 : (i + 1) * 128, :])
    for i in range(PART // 256):
        qkv_turned[i * 256 : (i + 1) * 256, :] = jnp.transpose(qkv[:, i * 256 : (i + 1) * 256])


def deal_kernel(order, gate, up, down, *outs):
    for j, out in enumerate(outs):
        here = pl.ds(pl.multiple_of(order[j] * ROWS, ROWS), ROWS)
        out[:ROWS, :SLOT] = gate[here, :]
        out[:ROWS, SLOT:] = up[here, :]
        put_down(out, down[pl.ds(pl.multiple_of(order[j] * PIECE, 16), PIECE), :])


def slice_sum_kernel(term, a, b, c, own, gain, out):
    total = add(term[...], a[...], b[...], c[...])
    grad = total[:ROWS, :]
    for_gain = jnp.sum(grad * own[...].astype(F32), axis=1, keepdims=True)
    lane = lax.broadcasted_iota(jnp.int32, (ROWS, WIDE), 1)
    out[:ROWS, :] = jnp.where(lane == SLOT - 1, for_gain, grad * gain[...]).astype(BF)
    out[ROWS:, :] = total[ROWS:, :].astype(BF)


MB = 256


def mlp_kernel(meta, *refs):
    us, (cots, w_in, w_turned_in) = refs[:16], refs[16:19]
    u_out, hidden_out, gate_out, up_out, mine_out, other_out = refs[19:25]
    u, c, hidden, grad, res, w, w_turned, in_sem, out_sem = refs[25:]

    def rows_of(i, n):
        return pl.ds(pl.multiple_of(i * n, n), n)

    loads = [
        pltpu.make_async_copy(w_in, w, in_sem.at[32]),
        pltpu.make_async_copy(w_turned_in, w_turned, in_sem.at[33]),
    ]
    for load in loads:
        load.start()
    for r in range(16):
        here = pl.ds(r * TOK, TOK)
        pltpu.make_async_copy(us[r], u.at[here, :], in_sem.at[r]).start()
        pltpu.make_async_copy(cots.at[rows_of(meta[r], TOK), :], c.at[here, :], in_sem.at[16 + r]).start()
    for load in loads:
        load.wait()

    def results(i):
        rows = rows_of(i, MB)
        return [
            pltpu.make_async_copy(u.at[rows, :], u_out.at[rows, :], out_sem.at[7 * i]),
            pltpu.make_async_copy(grad.at[rows, pl.ds(0, SLOT)], gate_out.at[rows, :], out_sem.at[7 * i + 1]),
            pltpu.make_async_copy(grad.at[rows, pl.ds(SLOT, SLOT)], up_out.at[rows, :], out_sem.at[7 * i + 5]),
        ] + [
            pltpu.make_async_copy(
                hidden.at[rows_of(2 * i + h, TOK), :],
                hidden_out.at[rows_of(meta[2 * i + h], TOK), :],
                out_sem.at[7 * i + 2 + h],
            )
            for h in range(2)
        ]

    def last(i, to):
        return pltpu.make_async_copy(res.at[rows_of(i, MB), :], to.at[rows_of(lax.rem(i, 4), MB), :], out_sem.at[7 * i + 4])

    def step(i, _):
        for h in range(2):
            rows = rows_of(2 * i + h, TOK)
            pltpu.make_async_copy(us[0], u.at[rows, :], in_sem.at[2 * i + h]).wait()
            pltpu.make_async_copy(us[0], c.at[rows, :], in_sem.at[16 + 2 * i + h]).wait()
        rows = rows_of(i, MB)
        x = u[rows, :]
        gate = dot(x, w[:, :SLOT])
        upward = dot(x, w[:, SLOT : 2 * SLOT])
        back = dot(c[rows, :], w[:, 2 * SLOT :])
        sig = jax.nn.sigmoid(gate)
        swished = gate * sig
        hidden[rows, :] = (swished * upward).astype(BF)
        grad[rows, :SLOT] = (back * upward * sig * (1.0 + gate * (1.0 - sig))).astype(BF)
        grad[rows, SLOT:] = (back * swished).astype(BF)
        for one in results(i):
            one.start()
        res[rows, :] = dot(grad[rows, :], w_turned[...]).astype(BF)

        @pl.when(i < 4)
        def _():
            last(i, mine_out).start()

        @pl.when(i >= 4)
        def _():
            last(i, other_out).start()

        return 0

    lax.fori_loop(0, SEQ // MB, step, 0)

    def finish(i, _):
        for one in results(i):
            one.wait()
        last(i, mine_out).wait()
        return 0

    lax.fori_loop(0, SEQ // MB, finish, 0)


def mlp(meta, us, cots, w, w_turned):
    return call(
        mlp_kernel,
        [sds((SEQ, D))] + [sds((SEQ, SLOT))] * 3 + [sds((SEQ // 2, D))] * 2,
        [SCALARS] + [ANYWHERE] * 19,
        25,
        out_specs=[ANYWHERE] * 6,
        scratch_shapes=[
            pltpu.VMEM((SEQ, D), BF),
            pltpu.VMEM((SEQ, D), BF),
            pltpu.VMEM((SEQ, SLOT), BF),
            pltpu.VMEM((SEQ, 2 * SLOT), BF),
            pltpu.VMEM((SEQ, D), BF),
            pltpu.VMEM((D, 3 * SLOT), BF),
            pltpu.VMEM((2 * SLOT, D), BF),
            pltpu.SemaphoreType.DMA((34,)),
            pltpu.SemaphoreType.DMA((56,)),
        ],
    )(meta, *us, cots, w, w_turned)


def through_down_kernel(order, hidden, w, mine, other):
    def step(i, _):
        rows = [hidden[pl.ds(pl.multiple_of(order[2 * i + h] * TOK, TOK), TOK), :] for h in range(2)]
        result = dot(jnp.concatenate(rows, axis=0), w[...]).astype(BF)
        there = pl.ds(pl.multiple_of(lax.rem(i, 4) * MB, MB), MB)

        @pl.when(i < 4)
        def _():
            mine[there, :] = result

        @pl.when(i >= 4)
        def _():
            other[there, :] = result

        return 0

    lax.fori_loop(0, SEQ // MB, step, 0)


def through_down(order, hidden, w):
    return call(through_down_kernel, [sds((SEQ // 2, D)), sds((SEQ // 2, D))], [SCALARS, WHOLE, WHOLE], 8)(
        order, hidden, w
    )


def gate_up_kernel(slots, *refs):
    held, gate, up, gain = refs
    total = jnp.zeros((gain.shape[0], HEAD), F32)
    for s in range(16):
        block = held[slots[s]]
        for i, out in enumerate((gate, up)):
            wide = block[:, i * SLOT : (i + 1) * SLOT].astype(F32)
            for j in range(NFS):
                at = j * (FF // NFS) + s * BLOCK
                out[:, at : at + BLOCK] = wide[:, j * PIECE : j * PIECE + BLOCK]
        total += block[:, SLOT - HEAD : SLOT].astype(F32)
    gain[...] = total


def gate_up_out(slots, parts):
    step = 32
    return pl.pallas_call(
        gate_up_kernel,
        grid_spec=pltpu.PrefetchScalarGridSpec(
            num_scalar_prefetch=1,
            grid=(ROWS // step,),
            in_specs=[pl.BlockSpec((NCTX, step, WIDE), lambda i, s: (0, i, 0))],
            out_specs=[
                pl.BlockSpec((step, FF), lambda i, s: (i, 0)),
                pl.BlockSpec((step, FF), lambda i, s: (i, 0)),
                pl.BlockSpec((step, HEAD), lambda i, s: (i, 0)),
            ],
        ),
        out_shape=[sds((ROWS, FF), F32), sds((ROWS, FF), F32), sds((ROWS, HEAD), F32)],
        compiler_params=pltpu.CompilerParams(vmem_limit_bytes=VMEM_BYTES),
        cost_estimate=pl.CostEstimate(flops=10000000000, bytes_accessed=1000000, transcendentals=0),
    )(slots, parts)


def down_kernel(slots, parts, out):
    for s in range(16):
        rows = take_down(parts.at[slots[s]], 0).astype(F32)
        out[s * BLOCK : (s + 1) * BLOCK, :] = rows[:BLOCK]


def down_out(slots, parts):
    below = SEND_ROWS - ROWS
    return pl.pallas_call(
        down_kernel,
        grid_spec=pltpu.PrefetchScalarGridSpec(
            num_scalar_prefetch=1,
            grid=(1,),
            in_specs=[pl.BlockSpec((NCTX, below, WIDE), lambda i, s: (0, ROWS // below, 0))],
            out_specs=pl.BlockSpec((FF // NFS, D), lambda i, s: (0, 0)),
        ),
        out_shape=sds((FF // NFS, D), F32),
        compiler_params=pltpu.CompilerParams(vmem_limit_bytes=VMEM_BYTES),
        cost_estimate=pl.CostEstimate(flops=7000000000, bytes_accessed=1000000, transcendentals=0),
    )(slots, parts)


def angle_tables():
    freqs = THETA ** (-(np.arange(HEAD // 2) * 2.0 / HEAD))
    angle = np.arange(SEQ)[:, None] * np.concatenate([freqs, freqs])[None, :]
    turn = np.where(np.arange(HEAD) < HEAD // 2, -1.0, 1.0)[None, :]
    return jnp.asarray(np.cos(angle), F32), jnp.asarray(np.sin(angle) * turn, F32)


def on_device(
    inputs,
    segments,
    gain_attn,
    w_query,
    b_query,
    w_key,
    b_key,
    w_value,
    b_value,
    w_output,
    gain_mlp,
    w_gate,
    w_up,
    w_down,
    cotangent,
):
    c, f = lax.axis_index("context"), lax.axis_index("fsdp")
    x, yl, core, z, yh = split_place(c, f)
    rel_ctx = jnp.stack([((x + a) % 4) * 4 + (yl ^ b) * 2 + (core ^ k) for k in range(2) for a, b in REL8])
    rel_ctx = rel_ctx.astype(jnp.int32)
    rel_shard = [((z + a) % 4) * 2 + (yh ^ b) for a, b in REL8]
    meta = jnp.stack([core, c // 2, *rel_shard]).astype(jnp.int32)
    rel_line = meta[2:10]
    cosine, sine = angle_tables()
    gain_one = gain_attn.astype(F32)[:, None]
    gain_two = gain_mlp.astype(F32)[:, None]
    tokens, cot = inputs[0], cotangent[0]

    unit, piece = call(
        first_kernel,
        [sds((TOK + 16, D)), sds((ROWS + 16, PART + HALF))],
        [SCALARS] + [WHOLE] * 10,
        3,
        scratch_shapes=[pltpu.VMEM((8, D), F32), pltpu.VMEM((8, 256), F32)],
    )(
        jnp.stack([f, core]).astype(jnp.int32),
        tokens,
        segments,
        w_query,
        w_key,
        w_value,
        w_output,
        gain_one,
        b_query.astype(F32)[None],
        b_key.astype(F32)[None],
        b_value.astype(F32)[None],
    )
    mlp_piece, gu_own = call(
        slice_kernel,
        [sds((SEND_ROWS, WIDE)), sds((ROWS, WIDE))],
        [SCALARS] + [WHOLE] * 4,
        6,
        scratch_shapes=[pltpu.VMEM((ROWS, WIDE), F32)],
    )((c ^ (2 * yh))[None].astype(jnp.int32), w_gate, w_up, w_down, gain_two)
    got, _ = together(gather_one(piece, SLICES) + [(unit, "core")])
    one, unit_other = got[:3], got[3]
    cots = lax.all_gather(after(cot, *got), "context", axis=0, tiled=True)
    two, (mlp_piece, gu_own) = together([(one[2], "z+"), (one[1], "z-")], mlp_piece, gu_own)
    got, _ = together([(one[2], "z-"), (two[0], "z+"), (mlp_piece, "yw")])
    two, three, m_pair = [*two, got[0]], got[1:2], got[2]

    q, kv, w_part, units = call(
        project_kernel,
        [sds((GROUP * CHIP, HEAD)), sds((8, CHIP + 16, 2 * HEAD)), sds((D, PART)), sds((CHIP, D))],
        [SCALARS] + [WHOLE] * 12,
        5,
    )(meta, unit, unit_other, piece, *one, *two, *three, cosine, sine)
    all_kv = over_chips(kv)
    m_one = [send(after(mlp_piece, kv), "z+"), send(after(mlp_piece, kv), "z-")]

    rows = sds((GROUP * CHIP, HEAD), F32)
    att, wide, lse, k, v, cuts = call(
        fwd_kernel,
        [sds((CHIP, HALF)), rows, rows, sds((SEQ, HEAD)), sds((SEQ, HEAD)), sds((2,), jnp.int32)],
        [SCALARS] + [WHOLE] * 2,
        20,
        out_specs=[WHOLE] * 5 + [SCALARS],
        scratch_shapes=[pltpu.VMEM((GROUP * CHIP, HEAD), F32)] * 3,
    )(meta, q, all_kv)

    _, (att, *m_one) = together([], att, *m_one)
    m_one = [*m_one, m_pair]
    m_two = [send(value, move) for value, move in gather_two(m_one, SLICES)]
    (att_other,), _ = together([(att, "core")])
    res_mine, res_theirs, atts, wo_turned = call(
        out_kernel,
        [sds((TOK, HALF), F32), sds((TOK, HALF), F32), sds((CHIP, D)), sds((HALF, D))],
        [SCALARS] + [WHOLE] * 10,
        4,
        scratch_shapes=[pltpu.VMEM((D, HALF), BF), pltpu.VMEM((CHIP, HALF), F32)],
    )(meta, att, att_other, piece, *one, *two, *three)
    (res_got,), _ = together([(res_theirs, "core")])
    residual, unit_two = call(
        residual_kernel, [sds((TOK, D), F32), sds((TOK, D))], [SCALARS] + [WHOLE] * 3, 2
    )(meta, tokens, res_mine, res_got)
    _, (unit_two, cots, *m_two) = together([], unit_two, cots, *m_two)

    got, _ = together(gather_one(unit_two, CTX) + gather_three(m_two, SLICES) + [(unit_two, "core")])
    one, m_three, other = got[:3], got[3:4], got[4:]
    got, _ = together(gather_two(one, CTX) + [(p, "core") for p in one])
    two, other = got[:3], other + got[3:6]
    w, w_turned, w_d, w_part_turned = call(
        weights_kernel,
        [sds((D, 3 * SLOT)), sds((2 * SLOT, D)), sds((SLOT, D)), sds((PART, D))],
        [SCALARS] + [WHOLE] * 9,
        10,
    )(rel_line, mlp_piece, *m_one, *m_two, *m_three, w_part)
    got, (w, w_turned) = together(gather_three(two, CTX) + [(p, "core") for p in two], w, w_turned)
    three, other = got[:1], other + got[1:4]
    twos = [unit_two, *one, *two, *three, *other, send(three[0], "core")]

    u2, hidden, grad_gate, grad_up, gnt_mine, gnt_other = mlp(rel_ctx, twos, cots, w, w_turned)

    got, _ = together([(gnt_other, "core")])
    q_two = pair_sum(gnt_mine, got[0])
    dw_gate = times_first(after(u2, *got), grad_gate).astype(BF)
    one, (dw_gate,) = together(sum_one(q_two, CTX), dw_gate)
    dw_up = times_first(u2, after(grad_up, *one)).astype(BF)
    two, (dw_up,) = together(sum_two(q_two, one, CTX), dw_up)
    dw_d = times_first(after(hidden, *two), cots).astype(BF)
    dealt = call(deal_kernel, [sds((SEND_ROWS, WIDE))] * 8, [SCALARS] + [WHOLE] * 3, 5)(
        rel_line, dw_gate, dw_up, dw_d
    )
    three, dealt = together(sum_three(q_two, one, two, CTX), *dealt)
    q_mlp = dealt.__getitem__

    s_one = [send(value, move) for value, move in sum_one(q_mlp, SLICES)]
    grad_residual, gao_mine, gao_theirs = call(
        norm_two_kernel,
        [sds((TOK, D), F32), sds((TOK, HALF)), sds((TOK, HALF))],
        [SCALARS] + [WHOLE] * 6,
        2,
        scratch_shapes=[pltpu.VMEM((TOK, D), BF)],
    )(meta, q_two(0), two[2], three[0], three[1], residual, cot)
    (gao_got,), _ = together([(gao_theirs, "core")])
    ga_mine, ga_theirs, gaos = call(
        out_grad_kernel,
        [sds((CHIP, HALF), F32), sds((CHIP, HALF)), sds((CHIP, HALF))],
        [SCALARS] + [WHOLE] * 3,
        3,
        scratch_shapes=[pltpu.VMEM((CHIP, D), F32)],
    )(meta, gao_mine, gao_got, wo_turned)
    (ga_got,), _ = together([(ga_theirs, "core")])

    stacked = pltpu.VMEM((GROUP * CHIP, HEAD), F32)
    dq, dkv = call(
        bwd_kernel,
        [sds((CHIP, HALF)), sds((SEQ, 2 * HEAD))],
        [SCALARS] * 2 + [WHOLE] * 9,
        28,
        scratch_shapes=[
            pltpu.VMEM((GROUP * CHIP, HEAD), BF),
            stacked,
            pltpu.VMEM((GROUP * CHIP, BK), BF),
            pltpu.VMEM((GROUP * CHIP, BK), BF),
            stacked,
            pltpu.VMEM((SEQ, HEAD), F32),
            pltpu.VMEM((SEQ, HEAD), F32),
        ],
    )(meta, cuts, q, k, v, wide, lse, cosine, sine, ga_mine, ga_got)
    _, (dq, dkv, *s_one) = together([], dq, dkv, *s_one)
    s_two = [send(value, move) for value, move in sum_two(q_mlp, s_one, SLICES)]

    all_dkv = over_chips(dkv)
    down_mine, down_other = through_down(rel_ctx, after(hidden, dkv), w_d)
    _, (all_dkv, down_mine, down_other, *s_two) = together([], all_dkv, down_mine, down_other, *s_two)
    s_three = [send(value, move) for value, move in sum_three(q_mlp, s_one, s_two, SLICES)]
    down_got = send(down_other, "core")

    gu1_mine, gu1_theirs, *pieces = call(
        project_grad_kernel,
        [sds((TOK, D), F32), sds((TOK, D))] + [sds((ROWS + 16, PART + HALF))] * 8,
        [SCALARS] + [WHOLE] * 8,
        9,
        scratch_shapes=[pltpu.VMEM((CHIP, PART), BF), pltpu.VMEM((D, PART + HALF), BF), pltpu.VMEM((CHIP, D), F32)],
    )(meta, all_dkv, dq, units, w_part_turned, cosine, sine, atts, gaos)

    _, (down_got, *pieces) = together([], down_got, *pieces)
    q_attn, q_down = pieces.__getitem__, pair_sum(down_mine, down_got)
    mine = call(slice_sum_kernel, sds((SEND_ROWS, WIDE)), [WHOLE] * 6, 3)(
        q_mlp(0), s_two[2], *s_three, gu_own, gain_two
    )
    got, (mine,) = together(sum_one(q_attn, SLICES) + [(gu1_theirs, "core")] + sum_one(q_down, CTX), mine)
    a_one, d_one = got[:2], got[3:]
    mlp_grads = lax.all_gather(mine, "context", axis=0)
    grad_tokens = call(norm_one_kernel, sds((TOK, D)), [WHOLE] * 4, 2)(gu1_mine, got[2], tokens, grad_residual)
    a_two, (grad_tokens,) = together(sum_two(q_attn, a_one, SLICES), grad_tokens)
    got, _ = together(sum_three(q_attn, a_one, a_two, SLICES) + sum_two(q_down, d_one, CTX))
    a_three, d_two = got[:2], got[2:]

    dealt = call(
        line_deal_kernel,
        sds((8, ROWS + 16, 2 * HEAD)),
        [WHOLE] * 4,
        3,
        scratch_shapes=[pltpu.VMEM((ROWS + 16, PART + HALF), F32)],
    )(q_attn(0), a_two[2], *a_three)
    blocks = over_chips(dealt)
    slots = jnp.arange(NCTX, dtype=jnp.int32) ^ (2 * yh)
    _, (blocks,) = together([], blocks)
    block = call(block_kernel, sds((8, ROWS + 16, 2 * HEAD)), [SCALARS] + [WHOLE] * 5, 2)(
        meta, blocks, w_query, w_key, w_value, gain_one
    )

    attn_mine = over_chips(block)
    grad_gate_w, grad_up_w, gain_two_cols = gate_up_out(slots, after(mlp_grads, block))
    grad_down_w = down_out(slots, after(mlp_grads, block))
    d_three = [send(after(value, block), move) for value, move in sum_three(q_down, d_one, d_two, CTX)]
    output = (residual + sum_all(q_down, d_two, d_three)).astype(BF)
    _, (attn_mine, grad_gate_w, grad_down_w) = together([], attn_mine, grad_gate_w, grad_down_w)
    attn_other = send(attn_mine, "core")

    grad_wq, grad_wk, grad_wv, grad_wo, sum_bq, sum_bk, sum_bv, grad_gain_one = call(
        attn_kernel,
        [
            sds((ROWS, D), F32),
            sds((ROWS, 256), F32),
            sds((ROWS, 256), F32),
            sds((ROWS, D), F32),
            sds((1, ROWS), F32),
            sds((1, 32), F32),
            sds((1, 32), F32),
            sds((1, ROWS), F32),
        ],
        [SCALARS, WHOLE, WHOLE],
        4,
        scratch_shapes=[
            pltpu.VMEM((8, D), F32),
            pltpu.VMEM((2, 8, 256), F32),
        ],
    )(jnp.stack([f, core]).astype(jnp.int32), attn_mine, attn_other)
    return (
        output[None],
        grad_tokens[None],
        grad_gain_one[0],
        grad_wq,
        sum_bq[0],
        grad_wk,
        sum_bk[0],
        grad_wv,
        sum_bv[0],
        grad_wo,
        gain_two_cols[:, HEAD - 1],
        grad_gate_w,
        grad_up_w,
        grad_down_w,
    )


def solution(mesh):
    tokens = P("fsdp", "context", None)
    matrix, vector = P("fsdp", None), P("fsdp")
    weights = (vector, matrix, vector, matrix, vector, matrix, vector, matrix, vector, matrix, matrix, matrix)
    return jax.shard_map(
        on_device,
        mesh=mesh,
        in_specs=(tokens, P("fsdp", "context"), *weights, tokens),
        out_specs=(tokens, tokens, *weights),
        check_vma=False,
    )
```
